128 devices in a mesh: ctx: 32 (over y, z, core), head: 4 (over x).
Axes of the slice: x: 4, y: 4, z: 4, core: 2. Of those that a mesh axis runs over, the one named last changes fastest.
Arguments:
- hidden: bfloat16 [4096, 2304], P('ctx'), may hold values from -6 to 6
- proj_weight: bfloat16 [3, 2304, 4096], P(None, None, 'head'), may hold values from -0.125 to 0.125
- conv_weight: float32 [3, 4, 4096], P(None, None, 'head'), may hold values from -3 to 3
- log_decay: float32 [4096, 4096], P('ctx', 'head'), may hold values from -1 to 0, as said below
- write_beta: float32 [4096, 32], P('ctx', 'head'), may hold values from 0 to 1, as said below
- saved_state: float32 [32, 32, 128, 128], P('ctx', 'head'), may hold values from -3 to 3
- output_grad: bfloat16 [4096, 4096], P('ctx', 'head'), may hold values from -6 to 6
- doc_lengths: int32 [8], replicated, may hold values from 1 to 2048, 4096 in all
Outputs:
- weight_grads: float32 [2304, 3, 4096], P('ctx', None, 'head')
- input_grad: bfloat16 [4096, 2304], P(('ctx', 'head'))
- decay_grad: float32 [4096, 4096], P('ctx', 'head')
The draws below stay inside these ranges and needn't reach their ends.
Inputs may be any that keep to these rules, and one draw needn't show every extreme that they name: `doc_lengths`: the 8 lengths sum to 4096, and the longest is exactly half of 4096. `log_decay`: every entry is negative. `write_beta`: every entry is positive and below one.
All inputs are finite; a program needn't handle non-finite values.
Results may differ from the reference program's by a relative error of at most 0.02.
Values may be sent and summed in bfloat16 or wider, within the bound.
A program may use at most 192 MiB of HBM per device.

```python
import math
import jax
import jax.numpy as jnp
import numpy as np
from jax import lax

D = 2304
H = 32
DK = 128
CONV = 4
TOK = 128
SPAN = 64
DOCS = 8
HC = 4096
TOKEN_TOTAL = 4096
SHARDS = 32


def draw_log_decay(key, part):
    key = jax.random.fold_in(key, 11)
    key_sequence = jax.random.split(key, 7)
    channel_rate = jnp.exp(jax.random.uniform(key_sequence[0], (1, H * DK), minval=math.log(3e-05), maxval=math.log(0.03)))
    scale_factor = jnp.exp(jax.random.uniform(key_sequence[3], (TOKEN_TOTAL // TOK, 1, H * DK), minval=-math.log(2.0), maxval=math.log(2.0)))
    scale_factor = jnp.broadcast_to(scale_factor, (TOKEN_TOTAL // TOK, TOK, H * DK)).reshape(TOKEN_TOTAL, H * DK)
    random_noise = jax.random.uniform(key_sequence[4], (TOKEN_TOTAL, H * DK), minval=0.5, maxval=1.5)
    spike_position = jax.random.randint(key_sequence[5], (4,), 0, TOKEN_TOTAL)
    spike_length = jax.random.uniform(key_sequence[6], (4,), minval=0.22, maxval=0.69)
    token_labels = jnp.arange(TOKEN_TOTAL, dtype=jnp.int32)
    spike_loss = jnp.max(jnp.where(token_labels[:, None] == spike_position[None, :], spike_length[None, :], 0.0), axis=1)
    return (-(channel_rate * scale_factor * random_noise + spike_loss[:, None])).astype(jnp.float32)


def draw_write_beta(key, part):
    key = jax.random.fold_in(key, 23)
    level_key, jitter_key = jax.random.split(key)
    head_level = jnp.exp(jax.random.uniform(level_key, (1, H), minval=math.log(0.003), maxval=math.log(0.5)))
    random_noise = jax.random.uniform(jitter_key, (TOKEN_TOTAL, H), minval=0.5, maxval=1.5)
    return (head_level * random_noise).astype(jnp.float32)


def block_scale(stream_key, shape, cuts, low, high):
    def one(dim, parts):
        draws = jax.random.uniform(jax.random.fold_in(jax.random.fold_in(stream_key, 6), dim), (parts,), jnp.float32, low / len(cuts), high / len(cuts))
        return jnp.repeat(jnp.exp(draws), shape[dim] // parts).reshape((-1,) + (1,) * (len(shape) - dim - 1))

    factor_of = one(*cuts[0])
    for cut in cuts[1:]:
        factor_of = factor_of * one(*cut)
    return factor_of


def length_profile(number_of, total, bound, lean):
    loads = [(1 << 20) // math.isqrt(rank ** lean) + 1 for rank in range(2, number_of + 1)]
    rest, holding = total - bound - (number_of - 1), [1] * (number_of - 1)
    while rest > 0:
        free = [i for i in range(number_of - 1) if holding[i] < bound]
        mass, left = sum([loads[i] for i in free]), rest
        for i in free:
            addition = min(bound - holding[i], max(1, left * loads[i] // mass), rest)
            holding[i] = holding[i] + addition
            rest = rest - addition
    return np.array([bound] + holding)


def ragged(stream_key, amount, total, most, skew):
    if amount == 2:
        one = jax.random.randint(stream_key, (), max(1, total - most), min(most, total - 1) + 1)
        return jnp.stack([one, total - one])
    lengths = jnp.asarray(length_profile(amount, total, most, skew), jnp.int32)
    couples = (amount - 1) // 2
    source_of, receiver = lengths[1:1 + 2 * couples:2], lengths[2:2 + 2 * couples:2]
    slack = jnp.minimum(source_of - 1, most - receiver)
    shifted = jax.random.randint(jax.random.fold_in(stream_key, 1), (couples,), 0, 1 << 20) % (slack + 1)
    lengths = lengths.at[1:1 + 2 * couples:2].set(source_of - shifted).at[2:2 + 2 * couples:2].set(receiver + shifted)
    return lengths[jax.random.permutation(jax.random.fold_in(stream_key, 2), amount)]


def centred(own_key, dims, deviation, bound, cuts=(), kind=jnp.bfloat16):
    drawn = jax.random.normal(own_key, dims, jnp.float32) * deviation
    if len(cuts) > 0:
        drawn = block_scale(own_key, dims, cuts, -0.22, 0.18) * drawn
    return jnp.clip(drawn, min=-bound, max=bound).astype(kind)


def setup_inputs(seed: int = 0) -> dict:
    key_of = jax.random.split(jax.random.key(seed), 9)
    return {
        "hidden": centred(key_of[0], (TOKEN_TOTAL, D), 1.0, 6.0, ((0, 32),)),
        "proj_weight": centred(key_of[1], (3, D, HC), D ** -0.5, 0.125, ((2, 4),)),
        "conv_weight": centred(key_of[2], (3, CONV, HC), 0.5, 3.0, ((2, 4),), jnp.float32),
        "log_decay": draw_log_decay(jax.random.fold_in(key_of[8], 71), 0),
        "write_beta": draw_write_beta(jax.random.fold_in(key_of[8], 71), 0),
        "saved_state": centred(key_of[5], (SHARDS, H, DK, DK), 0.5, 3.0, ((0, 32), (1, 4)), jnp.float32),
        "output_grad": centred(key_of[6], (TOKEN_TOTAL, HC), 1.0, 6.0, ((0, 32), (1, 4))),
        "doc_lengths": ragged(key_of[7], DOCS, TOKEN_TOTAL, TOKEN_TOTAL // 2, 2).astype(jnp.int32),
    }


EPSILON = 1e-06
TOP_PRECISION = lax.Precision.HIGHEST

def doc_starts(doc_lengths, positions):
    starts = jnp.cumsum(doc_lengths, dtype=jnp.int32) - doc_lengths
    before = starts[None, :] <= positions[:, None]
    return lax.optimization_barrier(jnp.max(jnp.where(before, starts[None, :], 0), axis=1)).astype(jnp.int32)

def features(extended, conv_weight, seg_start, positions, head_count):
    tap_count = conv_weight.shape[1]
    tok_rows = positions.shape[0]
    mixed = jnp.zeros((extended.shape[0], tok_rows, extended.shape[2]), extended.dtype)
    for offset in range(tap_count):
        first_row = tap_count - 1 - offset
        window = extended[:, first_row:first_row + tok_rows, :]
        usable = (positions - offset >= seg_start).astype(extended.dtype)
        mixed = mixed + window * conv_weight[:, offset, :][:, None, :] * usable[None, :, None]
    active = jax.nn.silu(mixed)
    shaped = active.reshape(3, tok_rows, head_count, -1)
    paired = shaped[:2]
    normed = paired / jnp.sqrt(lax.optimization_barrier(jnp.sum(paired * paired, axis=-1, keepdims=True)) + EPSILON)
    scaled = normed[0] * shaped.shape[-1] ** (-0.5)
    return (scaled, normed[1], shaped[2])

def span_step(incoming_state, queries, keys_in, values, log_decay, beta_rows, seg_start, positions):
    block_len = queries.shape[0]
    summed = jnp.cumsum(log_decay, axis=0)
    growth = jnp.exp(summed)
    shrink = jnp.exp(-summed)
    key_shifted_up = keys_in * growth
    key_minus = keys_in * shrink
    query_shifted_up = queries * growth
    leading_part = (seg_start < positions[0]).astype(growth.dtype)
    same_doc = (seg_start[:, None] == seg_start[None, :]).astype(growth.dtype)
    strict = jnp.tril(jnp.ones((block_len, block_len), growth.dtype), -1)
    inclusive = jnp.tril(jnp.ones((block_len, block_len), growth.dtype))
    coupling = jnp.einsum('thk,shk->hts', key_shifted_up, key_minus, precision=TOP_PRECISION) * (same_doc * strict)[None]
    reading = jnp.einsum('thk,shk->hts', query_shifted_up, key_minus, precision=TOP_PRECISION) * (same_doc * inclusive)[None]
    beta_heads = beta_rows.T
    system = jnp.eye(block_len, dtype=growth.dtype)[None] + beta_heads[:, :, None] * coupling
    recalled_value = jnp.einsum('fju,jul->jfl', key_shifted_up, incoming_state, precision=TOP_PRECISION) * leading_part[None, :, None]
    target = beta_heads[:, :, None] * (jnp.transpose(values, (1, 0, 2)) - recalled_value)
    written_value = lax.linalg.triangular_solve(system, target, left_side=True, lower=True, unit_diagonal=True)
    layer_output = jnp.einsum('nwj,wjl->nwl', query_shifted_up, incoming_state, precision=TOP_PRECISION) * leading_part[:, None, None]
    layer_output = layer_output + jnp.einsum('hts,hsv->thv', reading, written_value, precision=TOP_PRECISION)
    final_decay = growth[-1]
    carried_over = key_minus * final_decay[None] * same_doc[-1][:, None, None]
    outgoing_state = incoming_state * (final_decay * leading_part[-1])[:, :, None]
    outgoing_state = outgoing_state + jnp.einsum('pge,gpu->geu', carried_over, written_value, precision=TOP_PRECISION)
    return (layer_output, outgoing_state)

def recurrence(queries, keys_in, values, log_decay, beta_rows, incoming_state, seg_start, positions):
    tok_rows, head_count, head_width = queries.shape
    blocks = tok_rows // SPAN

    def blocked(source):
        return source.reshape((blocks, SPAN) + source.shape[1:])
    decay_rows = log_decay.reshape(tok_rows, head_count, head_width)
    inputs = (blocked(queries), blocked(keys_in), blocked(values), blocked(decay_rows), blocked(beta_rows), blocked(seg_start), blocked(positions))

    def advance(state_now, block_in):
        layer_output, outgoing_state = span_step(state_now, *block_in)
        return (outgoing_state, layer_output)
    final_state, outputs = lax.scan(advance, incoming_state, inputs)
    return (outputs.reshape(tok_rows, head_count, head_width), final_state)

def reference(hidden, proj_weight, conv_weight, log_decay, write_beta, saved_state, output_grad, doc_lengths):
    positions = jnp.arange(TOKEN_TOTAL, dtype=jnp.int32)
    seg_start = doc_starts(doc_lengths, positions)
    projected = jnp.stack([jnp.dot(hidden.astype(jnp.float32), proj_weight[matrix].astype(jnp.float32), preferred_element_type=jnp.float32) for matrix in range(3)]).astype(jnp.bfloat16)
    padding = jnp.zeros((3, CONV - 1, H * DK), jnp.float32)
    extended = jnp.concatenate([padding, projected.astype(jnp.float32)], axis=1)

    def shaped_features(source):
        return features(source, conv_weight, seg_start, positions, H)
    feature_set, feature_pull = jax.vjp(shaped_features, extended)

    def by_shard(source):
        return source.reshape((SHARDS, TOK) + source.shape[1:])
    out_grad = output_grad.astype(jnp.float32).reshape(TOKEN_TOTAL, H, DK)
    inputs = (by_shard(feature_set[0]), by_shard(feature_set[1]), by_shard(feature_set[2]), by_shard(log_decay), by_shard(write_beta), saved_state, by_shard(out_grad), by_shard(seg_start), by_shard(positions))

    def backward(state_grad, shard_in):
        queries, keys_in, values, decay_rows, beta_rows, incoming_state, grad_rows, seg_rows, pos_rows = shard_in

        def local_chain(query_arg, key_arg, value_arg, decay_arg, state_arg):
            return recurrence(query_arg, key_arg, value_arg, decay_arg, beta_rows, state_arg, seg_rows, pos_rows)
        unused, chain_pull = jax.vjp(local_chain, queries, keys_in, values, decay_rows, incoming_state)
        pulled = chain_pull((grad_rows, state_grad))
        return (pulled[4], (pulled[0], pulled[1], pulled[2], pulled[3]))
    unused, pieces = lax.scan(backward, jnp.zeros((H, DK, DK), jnp.float32), inputs, reverse=True)
    query_grad = pieces[0].reshape(TOKEN_TOTAL, H, DK)
    key_grad = pieces[1].reshape(TOKEN_TOTAL, H, DK)
    value_grad = pieces[2].reshape(TOKEN_TOTAL, H, DK)
    decay_grad = pieces[3].reshape(TOKEN_TOTAL, H * DK)
    extended_grad = feature_pull((query_grad, key_grad, value_grad))[0]
    raw_grad = extended_grad[:, CONV - 1:, :].astype(jnp.bfloat16)

    def add_shard(total, shard):
        hidden_rows = lax.dynamic_slice_in_dim(hidden, shard * TOK, TOK, 0).astype(jnp.float32)
        grad_rows = lax.dynamic_slice_in_dim(raw_grad, shard * TOK, TOK, 1).astype(jnp.float32)
        partial_sum = jnp.einsum('td,ptc->dpc', hidden_rows, grad_rows, precision=TOP_PRECISION)
        rounded = lax.optimization_barrier(partial_sum.astype(jnp.bfloat16))
        return (total + rounded.astype(jnp.float32), None)
    weight_grads, unused = lax.scan(add_shard, jnp.zeros((D, 3, H * DK), jnp.float32), jnp.arange(SHARDS, dtype=jnp.int32))
    input_total = jnp.dot(raw_grad[0].astype(jnp.float32), proj_weight[0].T.astype(jnp.float32), preferred_element_type=jnp.float32)
    input_total = input_total + jnp.dot(raw_grad[1].astype(jnp.float32), proj_weight[1].T.astype(jnp.float32), preferred_element_type=jnp.float32)
    input_total = input_total + jnp.dot(raw_grad[2].astype(jnp.float32), proj_weight[2].T.astype(jnp.float32), preferred_element_type=jnp.float32)
    return (weight_grads, input_total.astype(jnp.bfloat16), decay_grad)
```

```python
import functools

import jax
import jax.numpy as jnp
from jax import lax
from jax.experimental import pallas as pl
from jax.experimental.pallas import tpu as pltpu
from jax.sharding import PartitionSpec as P

MESH = pl.DeviceIdType.MESH
F32, BF16 = jnp.float32, jnp.bfloat16
EPSILON = 1e-06
HEADS, TOK, DK, D = 8, 128, 128, 2304
ROW, ROWS = 8, 4
SLAB, PADDED = 72, 80
HALO = 16
NN, NT, TN = (((1,), (0,)), ((), ())), (((1,), (1,)), ((), ())), (((0,), (0,)), ((), ()))


def dot1(a, b, form=NN):
    return lax.dot_general(a.astype(BF16), b.astype(BF16), form, preferred_element_type=F32)


def split(a):
    high = a.astype(BF16)
    return high, (a - high.astype(F32)).astype(BF16)


def dot3(a, b, form=NN):
    (ah, al), (bh, bl) = split(a), split(b)
    (la,), (lb,) = form[0]
    left = jnp.concatenate([ah, al, ah], axis=la)
    right = jnp.concatenate([bh, bh, bl], axis=lb)
    return lax.dot_general(left, right, form, preferred_element_type=F32)


def dot_exact_left(a, b):
    bh, bl = split(b)
    return lax.dot_general(
        jnp.concatenate([a, a], axis=1), jnp.concatenate([bh, bl], axis=0), NN, preferred_element_type=F32
    )


def iota(dim):
    return lax.broadcasted_iota(jnp.int32, (TOK, TOK), dim)


def me():
    return lax.axis_index("ctx"), lax.axis_index("head")


def chain_kernel(
    doc_ref, hid_ref, w_ref, conv_ref, ld_ref, beta_ref, s0_ref, og_ref,
    raw_ref, dld_ref, ht_ref,
    xext, wbuf, pe, ht_t, ht_send, ht_recv, norm, val, inv, dsil, masks, bet,
    grow, shrink, tinv, read, mb, rx, pc, tot, ry, ds, rd, uu, wl, tk, dkm, gg,
    tail, spill, spill_in,
    w_sem, x_sem, halo_sem, ht_ssem, ht_rsem, mb_ssem, mb_rsem, ry_ssem, ry_rsem, ds_ssem, ds_rsem, sp_sem,
):
    ctx, head = me()
    row, col = ctx // ROW, lax.rem(ctx, ROW)
    after, before = lax.rem(ctx + 1, ROW * ROWS), lax.rem(ctx + ROW * ROWS - 1, ROW * ROWS)

    def w_copy(group):
        at = pl.ds(pl.multiple_of(group * 256, 256), 256)
        return pltpu.make_async_copy(w_ref.at[:, :, at], wbuf.at[:, :, at], w_sem.at[group])

    for group in range(4):
        w_copy(group).start()
    x_copy = pltpu.make_async_copy(hid_ref, xext.at[pl.ds(HALO, TOK)], x_sem)
    x_copy.start()

    barrier = pltpu.get_barrier_semaphore()
    for step in range(1, ROW):
        mate = row * ROW + lax.rem(col + step, ROW)
        pl.semaphore_signal(barrier, inc=1, device_id=(mate, head), device_id_type=MESH)
    for step in range(1, ROWS):
        mate = lax.rem(row + step, ROWS) * ROW + col
        pl.semaphore_signal(barrier, inc=1, device_id=(mate, head), device_id_type=MESH)
    for mate in (after, before):
        pl.semaphore_signal(barrier, inc=1, device_id=(mate, head), device_id_type=MESH)

    t, s = iota(0), iota(1)
    first = ctx * TOK
    seg_t, seg_s = jnp.zeros_like(t), jnp.zeros_like(s)
    seg_last, start = jnp.int32(0), jnp.int32(0)
    for doc in range(8):
        seg_t = jnp.where(t + first >= start, jnp.maximum(seg_t, start), seg_t)
        seg_s = jnp.where(s + first >= start, jnp.maximum(seg_s, start), seg_s)
        seg_last = jnp.where(first + TOK - 1 >= start, jnp.maximum(seg_last, start), seg_last)
        start = start + doc_ref[doc]
    same = seg_t == seg_s
    masks[0] = jnp.where(same & (t > s), 1.0, 0.0)
    masks[1] = jnp.where(same & (t >= s), 1.0, 0.0)
    masks[2] = jnp.where(seg_t < first, 1.0, 0.0)
    masks[3] = jnp.where(seg_t == seg_last, 1.0, 0.0)
    for offset in range(1, 4):
        masks[3 + offset] = jnp.where(t + first - offset >= seg_t, 1.0, 0.0)
    lead_last = jnp.where(seg_last < first, 1.0, 0.0)
    for h in range(HEADS):
        bet[h] = jnp.broadcast_to(beta_ref[:, h : h + 1], (TOK, TOK))

    pl.semaphore_wait(barrier, ROW - 1 + ROWS - 1 + 2)

    halo = pltpu.make_async_remote_copy(
        src_ref=hid_ref.at[pl.ds(TOK - HALO, HALO)], dst_ref=xext.at[pl.ds(0, HALO)],
        send_sem=halo_sem.at[0], recv_sem=halo_sem.at[1], device_id=(after, head), device_id_type=MESH,
    )
    halo.start()

    for tile in range(D // 128):
        ht_t[tile * 128 : tile * 128 + 128] = hid_ref[:, tile * 128 : tile * 128 + 128].astype(F32).T
    ht_t[D : D + 8] = jnp.zeros((8, TOK), F32)
    for owner in range(ROW):
        for part in range(ROWS):
            base = (part * ROW + owner) * SLAB
            ht_send[owner, part * PADDED : part * PADDED + PADDED] = ht_t[base : base + PADDED].astype(BF16)

    def ht_copy(step):
        mate = lax.rem(col + step, ROW)
        return pltpu.make_async_remote_copy(
            src_ref=ht_send.at[mate], dst_ref=ht_recv.at[:, pl.ds(pl.multiple_of(col * TOK, TOK), TOK)],
            send_sem=ht_ssem.at[step], recv_sem=ht_rsem.at[step],
            device_id=(row * ROW + mate, head), device_id_type=MESH,
        )

    for step in range(1, ROW):
        ht_copy(step).start()
    ht_recv[:, pl.ds(pl.multiple_of(col * TOK, TOK), TOK)] = ht_send[col]

    x_copy.wait()
    halo.wait()

    def project(group, carry):
        w_copy(group).wait()
        wide = pl.ds(pl.multiple_of(group * 256, 256), 256)
        for p in range(3):
            made = jnp.dot(xext[...], wbuf[p, :, wide], preferred_element_type=F32)
            pe[p, :, wide] = made.astype(BF16).astype(F32)
        for half in range(2):
            h = group * 2 + half
            lanes = pl.ds(pl.multiple_of(h * DK, DK), DK)
            for p in range(3):
                mixed = pe[p, pl.ds(HALO, TOK), lanes] * conv_ref[p, 0:1, lanes]
                for offset in range(1, 4):
                    tap = pe[p, pl.ds(HALO - offset, TOK), lanes] * conv_ref[p, offset : offset + 1, lanes]
                    mixed = mixed + tap * masks[3 + offset]
                gate = 1.0 / (1.0 + jnp.exp(-mixed))
                active = mixed * gate
                dsil[p, h] = gate * (1.0 + mixed * (1.0 - gate))
                if p == 2:
                    val[h] = active
                else:
                    scale = lax.rsqrt(jnp.sum(active * active, axis=1, keepdims=True) + EPSILON)
                    norm[p, h] = active * scale
                    inv[p, h] = jnp.broadcast_to(scale, (TOK, DK))
        return carry

    lax.fori_loop(0, 4, project, 0)

    def mb_copy(h):
        return pltpu.make_async_remote_copy(
            src_ref=mb.at[h], dst_ref=rx.at[col], send_sem=mb_ssem.at[h], recv_sem=mb_rsem.at[col],
            device_id=(row * ROW + h, head), device_id_type=MESH,
        )

    batch = 4

    def transition(step, carry):
        heads = [step * batch + k for k in range(batch)]
        lanes = [pl.ds(pl.multiple_of(h * DK, DK), DK) for h in heads]
        below = (iota(0) >= iota(1)).astype(F32).astype(BF16)
        summed = [dot_exact_left(below, ld_ref[:, lane]) for lane in lanes]
        mids = [x[63:64] for x in summed]
        ups = [jnp.exp(x - mid) for x, mid in zip(summed, mids)]
        downs = [jnp.exp(mid - x) for x, mid in zip(summed, mids)]
        for h, up, down, mid in zip(heads, ups, downs, mids):
            grow[h], shrink[h] = up, down
        keys = [norm[1, h] for h in heads]
        queries = [norm[0, h] * DK ** (-0.5) for h in heads]
        low = [k * x for k, x in zip(keys, downs)]
        high = [jnp.concatenate([k * x, q * x], axis=0) for k, q, x in zip(keys, queries, ups)]
        both = [dot3(a, b, NT) for a, b in zip(high, low)]
        ns = [jnp.where(masks[0] > 0, x[:TOK], 0.0) * bet[h] for x, h in zip(both, heads)]
        rs = [jnp.where(masks[1] > 0, x[TOK:], 0.0) for x in both]
        apart = iota(0) ^ iota(1)
        eye = (apart == 0).astype(F32)
        solved = [eye - jnp.where(apart == 1, n, 0.0) for n in ns]
        for level in range(1, 7):
            edge = [jnp.where((apart >> level) == 1, n, 0.0) for n in ns]
            edge = [dot3(e, x) for e, x in zip(edge, solved)]
            solved = [x - dot3(x, e) for e, x in zip(edge, solved)]
        for h, x, r in zip(heads, solved, rs):
            tinv[h], read[h] = x, r.astype(BF16)
        lead = masks[2]
        firsts = [jnp.exp(mid) for mid in mids]
        ups0 = [x * e * lead for x, e in zip(ups, firsts)]
        ws = [dot1(x, bet[h] * k * up) for x, h, k, up in zip(solved, heads, keys, ups0)]
        xs = [q * up - dot1(r, w) for q, up, r, w in zip(queries, ups0, rs, ws)]
        lasts = [jnp.exp(x[TOK - 1 :] - mid) for x, mid in zip(summed, mids)]
        ends = [x * last * masks[3] for x, last in zip(low, lasts)]
        for h, lane, w, x, end, last, e in zip(heads, lanes, ws, xs, ends, lasts, firsts):
            mb[h, :, 0:DK] = (eye * (last * e * lead_last) - dot1(w, end, TN)).astype(BF16)
            mb[h, :, DK:] = dot1(x, og_ref[:, lane], TN).astype(BF16)
            tk[h] = dot1(tinv[h], end, TN).astype(BF16)
        for h in heads:
            @pl.when(h != col)
            def _():
                mb_copy(h).start()
        return carry

    lax.fori_loop(0, HEADS // batch, transition, 0)
    rx[col] = mb[col]

    def shift_back(p, h, lane, grad_active):
        dmix = grad_active * dsil[p, h]
        t = iota(0)
        main = dmix * conv_ref[p, 0:1, lane]
        over = jnp.zeros((TOK, DK), F32)
        for offset in range(1, 4):
            part = dmix * masks[3 + offset] * conv_ref[p, offset : offset + 1, lane]
            part = pltpu.roll(part, TOK - offset, 0)
            inside = t < TOK - offset
            main = main + jnp.where(inside, part, 0.0)
            over = over + jnp.where(inside, 0.0, part)
        raw_ref[p, :, lane] = main.astype(BF16)
        tail[p, :, lane] = main[TOK - HALO :]
        spill[p, :, lane] = over[TOK - 8 :]

    def unnorm(p, h, grad):
        n = norm[p, h]
        return inv[p, h] * (grad - n * jnp.sum(n * grad, axis=1, keepdims=True))

    def local(step, carry):
        heads = [step * 2 + k for k in range(2)]
        for h in heads:
            lane = pl.ds(pl.multiple_of(h * DK, DK), DK)
            og = og_ref[:, lane]
            up, down = grow[h], shrink[h]
            first_e = jnp.exp(dot_exact_left((iota(1) < 64).astype(F32).astype(BF16), ld_ref[:, lane]))
            up0 = up * first_e * masks[2]
            q = norm[0, h] * DK ** (-0.5)
            k = norm[1, h]
            state = s0_ref[0, h].astype(BF16)
            recalled = dot1(k * up0, state)
            u = dot1(tinv[h], bet[h] * (val[h] - recalled)).astype(BF16)
            uu[h] = u
            dread = jnp.where(masks[1] > 0, dot1(og, u, NT), 0.0).astype(BF16)
            dq = dot1(dread, k * down) * up + dot1(og, state, NT) * up0
            dkm[h] = dot1(dread, q * up, TN)
            gg[h] = q * dq
            wl[h] = dot1(tinv[h], dot1(read[h], og, TN), TN)
            shift_back(0, h, lane, unnorm(0, h, dq * DK ** (-0.5)))
        return carry

    for j in range(ROW):
        @pl.when(j != col)
        def _():
            pltpu.make_async_remote_copy(
                src_ref=mb.at[j], dst_ref=rx.at[j], send_sem=mb_ssem.at[j], recv_sem=mb_rsem.at[j],
                device_id=(row * ROW + j, head), device_id_type=MESH,
            ).wait_recv()

    def compose(m, x, b):
        hi, lo = split(x)
        out = jnp.dot(m, jnp.concatenate([hi, lo], axis=1), preferred_element_type=F32)
        n = x.shape[1]
        return out[:, :n] + out[:, n:] + b

    x = rx[ROW - 1].astype(F32)
    pc[ROW - 2] = x
    zeros = jnp.zeros((DK, DK), F32)
    for j in range(ROW - 2, -1, -1):
        b = jnp.concatenate([zeros, rx[j, :, DK:].astype(F32)], axis=1)
        x = compose(rx[j, :, 0:DK], x, b)
        if j > 0:
            pc[j - 1] = x
    tot[...] = x.astype(BF16)

    def ry_copy(step):
        mate = lax.rem(row + step, ROWS) * ROW + col
        return pltpu.make_async_remote_copy(
            src_ref=tot, dst_ref=ry.at[ROWS - step], send_sem=ry_ssem.at[step], recv_sem=ry_rsem.at[step],
            device_id=(mate, head), device_id_type=MESH,
        )

    for step in range(1, ROWS):
        ry_copy(step).start()
    for step in range(1, ROWS):
        ry_copy(step).wait_recv()
    total = jnp.zeros((DK, DK), F32)
    for k in range(ROWS - 1, 0, -1):
        moved = compose(ry[k, :, 0:DK], total, ry[k, :, DK:].astype(F32))
        total = jnp.where(row + k < ROWS, moved, total)

    def ds_copy(j):
        return pltpu.make_async_remote_copy(
            src_ref=ds.at[j], dst_ref=rd.at[col], send_sem=ds_ssem.at[j], recv_sem=ds_rsem.at[col],
            device_id=(row * ROW + j, head), device_id_type=MESH,
        )

    total_b = total.astype(BF16)
    for j in range(ROW):
        if j == ROW - 1:
            ds[j] = total_b
        else:
            ds[j] = (dot1(pc[j, :, 0:DK], total_b) + pc[j, :, DK:]).astype(BF16)

        @pl.when(j != col)
        def _():
            ds_copy(j).start()

    rd[col] = ds[col]

    lax.fori_loop(0, HEADS // 2, local, 0)

    for j in range(ROW):
        @pl.when(j != col)
        def _():
            pltpu.make_async_remote_copy(
                src_ref=ds.at[j], dst_ref=rd.at[j], send_sem=ds_ssem.at[j], recv_sem=ds_rsem.at[j],
                device_id=(row * ROW + j, head), device_id_type=MESH,
            ).wait_recv()

    def carried(step, carry):
        heads = [step * 2 + k for k in range(2)]
        above = (iota(1) >= iota(0)).astype(F32).astype(BF16)
        ones = jnp.ones((8, DK), BF16)
        for h in heads:
            lane = pl.ds(pl.multiple_of(h * DK, DK), DK)
            up, down = grow[h], shrink[h]
            sums = dot_exact_left(
                jnp.where(iota(0) < 64, jnp.where(iota(1) < 64, 1.0, 0.0), jnp.where(iota(1) >= 64, 1.0, 0.0)).astype(BF16),
                ld_ref[:, lane],
            )
            first_e, last_e = jnp.exp(sums[0:1]), jnp.exp(sums[TOK - 1 :])
            lead = masks[2]
            k = norm[1, h]
            dnext = rd[h]
            state = s0_ref[0, h]
            u = uu[h]
            w = wl[h] + dot1(tk[h], dnext)
            bw = bet[h] * w
            da = jnp.where(masks[0] > 0, -dot1(bw, u, NT), 0.0).astype(BF16)
            dku = dot1(da, k * down) - dot1(bw * lead, state, NT) * first_e
            dkm_all = dkm[h] + dot1(da, k * up, TN)
            dend = dot1(u, dnext, NT) * last_e * masks[3]
            rising = dku * up
            ending = dend * down
            falling = dkm_all * down + ending
            dk = rising + falling
            dg = gg[h] + k * (rising - falling)
            crossed = state * dnext.astype(F32) * lead_last
            ch, cl = split(crossed)
            extra = dot1(ones, ch, NT) + dot1(ones, cl, NT)
            extra = extra[0:1] * first_e * last_e + jnp.sum(k * ending, axis=0, keepdims=True)
            dld_ref[:, lane] = dot_exact_left(above, dg) + extra
            shift_back(1, h, lane, unnorm(1, h, dk))
            shift_back(2, h, lane, bw)
        return carry

    lax.fori_loop(0, HEADS // 2, carried, 0)

    send = pltpu.make_async_remote_copy(
        src_ref=spill, dst_ref=spill_in, send_sem=sp_sem.at[0], recv_sem=sp_sem.at[1],
        device_id=(before, head), device_id_type=MESH,
    )
    send.start()
    for step in range(1, ROW):
        ht_copy(step).wait()
    ht_ref[...] = ht_recv[...]
    for step in range(1, ROWS):
        ry_copy(step).wait_send()
    for j in range(ROW):
        @pl.when(j != col)
        def _():
            mb_copy(j).wait_send()
            ds_copy(j).wait_send()
    send.wait()
    for p in range(3):
        low = tail[p, 8:16] + spill_in[p]
        raw_ref[p, TOK - HALO :, :] = jnp.concatenate([tail[p, 0:8], low], axis=0).astype(BF16)


def chain(doc_lengths, hidden, proj_weight, conv_weight, log_decay, write_beta, saved_state, output_grad):
    vm = pl.BlockSpec(memory_space=pltpu.VMEM)
    sq = (HEADS, TOK, DK)
    dma = pltpu.SemaphoreType.DMA
    return pl.pallas_call(
        chain_kernel,
        out_shape=(
            jax.ShapeDtypeStruct((3, TOK, HEADS * DK), BF16),
            jax.ShapeDtypeStruct((TOK, HEADS * DK), F32),
            jax.ShapeDtypeStruct((ROWS * PADDED, ROW * TOK), BF16),
        ),
        in_specs=[pl.BlockSpec(memory_space=pltpu.SMEM), vm, pl.BlockSpec(memory_space=pl.ANY), vm, vm, vm, vm, vm],
        out_specs=(vm, vm, vm),
        scratch_shapes=[
            pltpu.VMEM((HALO + TOK, D), BF16),
            pltpu.VMEM((3, D, HEADS * DK), BF16),
            pltpu.VMEM((3, HALO + TOK, HEADS * DK), F32),
            pltpu.VMEM((D + 8, TOK), F32),
            pltpu.VMEM((ROW, ROWS * PADDED, TOK), BF16),
            pltpu.VMEM((ROWS * PADDED, ROW * TOK), BF16),
            pltpu.VMEM((2,) + sq, F32),
            pltpu.VMEM(sq, F32),
            pltpu.VMEM((2,) + sq, F32),
            pltpu.VMEM((3,) + sq, F32),
            pltpu.VMEM((7, TOK, TOK), F32),
            pltpu.VMEM(sq, F32),
            pltpu.VMEM(sq, F32),
            pltpu.VMEM(sq, F32),
            pltpu.VMEM(sq, F32),
            pltpu.VMEM(sq, BF16),
            pltpu.VMEM((HEADS, DK, 2 * DK), BF16),
            pltpu.VMEM((ROW, DK, 2 * DK), BF16),
            pltpu.VMEM((ROW, DK, 2 * DK), F32),
            pltpu.VMEM((DK, 2 * DK), BF16),
            pltpu.VMEM((ROWS, DK, 2 * DK), BF16),
            pltpu.VMEM((ROW, DK, DK), BF16),
            pltpu.VMEM((HEADS, DK, DK), BF16),
            pltpu.VMEM(sq, BF16),
            pltpu.VMEM(sq, F32),
            pltpu.VMEM(sq, BF16),
            pltpu.VMEM(sq, F32),
            pltpu.VMEM(sq, F32),
            pltpu.VMEM((3, HALO, HEADS * DK), F32),
            pltpu.VMEM((3, 8, HEADS * DK), F32),
            pltpu.VMEM((3, 8, HEADS * DK), F32),
            dma((4,)), dma, dma((2,)), dma((ROW,)), dma((ROW,)), dma((ROW,)), dma((ROW,)),
            dma((ROWS,)), dma((ROWS,)), dma((ROW,)), dma((ROW,)), dma((2,)),
        ],
        compiler_params=pltpu.CompilerParams(
            collective_id=0, has_side_effects=True, vmem_limit_bytes=56 * 1024 * 1024
        ),
        cost_estimate=pl.CostEstimate(flops=4_000_000_000, bytes_accessed=18_000_000, transcendentals=1_000_000),
        name="chain",
    )(doc_lengths, hidden, proj_weight, conv_weight, log_decay, write_beta, saved_state, output_grad)


def grads_kernel(
    raw_ref, ht_ref, w_ref, wg_ref, ig_ref,
    wbuf, raws, part, psend, precv, ipart, isend, irecv,
    w_sem, own_sem, a_ssem, a_rsem, p_ssem, p_rsem, i_ssem, i_rsem,
):
    ctx, head = me()
    row, col = ctx // ROW, lax.rem(ctx, ROW)
    z, core = col // 2, lax.rem(col, 2)
    wide = HEADS * DK

    def device(zz, cc):
        return (row * ROW + lax.rem(zz, 4) * 2 + cc, head)

    def slot(zz, cc):
        return lax.rem(zz, 4) * 2 + cc

    up, down, twin = device(z + 1, core), device(z + 3, core), device(z, 1 - core)

    for p in range(3):
        pltpu.make_async_copy(w_ref.at[p], wbuf.at[p], w_sem.at[p]).start()

    barrier = pltpu.get_barrier_semaphore()
    for mate in (up, down, twin):
        pl.semaphore_signal(barrier, inc=1, device_id=mate, device_id_type=MESH)
    for step in range(1, 4):
        pl.semaphore_signal(
            barrier, inc=1, device_id=(lax.rem(row + step, ROWS) * ROW + col, head), device_id_type=MESH
        )
        pl.semaphore_signal(barrier, inc=1, device_id=(ctx, lax.rem(head + step, 4)), device_id_type=MESH)
    pl.semaphore_wait(barrier, 9)

    def rows_of(j):
        return pl.ds(pl.multiple_of(j * TOK, TOK), TOK)

    left, right = pl.ds(0, wide // 2), pl.ds(wide // 2, wide // 2)

    def gather(p, kind):
        mine = raw_ref.at[p]
        if kind == 0:
            src, dst, to = mine, raws.at[p, rows_of(slot(z, core))], up
        elif kind == 1:
            src, dst, to = mine, raws.at[p, rows_of(slot(z, core))], down
        elif kind == 2:
            src = dst = raws.at[p, rows_of(slot(z + 3, core)), left]
            to = up
        elif kind == 3:
            src = dst = raws.at[p, rows_of(slot(z + 1, core)), right]
            to = down
        elif kind == 4:
            src, dst, to = mine, raws.at[p, rows_of(slot(z, core))], twin
        else:
            src = dst = raws.at[p, rows_of(slot(z + (3, 1, 2)[kind - 5], core))]
            to = twin
        return pltpu.make_async_remote_copy(
            src_ref=src, dst_ref=dst, send_sem=a_ssem.at[p, kind], recv_sem=a_rsem.at[p, kind],
            device_id=to, device_id_type=MESH,
        )

    def own(p):
        return pltpu.make_async_copy(raw_ref.at[p], raws.at[p, rows_of(slot(z, core))], own_sem.at[p])

    for p in range(3):
        for kind in (0, 1, 4):
            gather(p, kind).start()
        own(p).start()

    def input_part(tile, carry):
        at = pl.ds(pl.multiple_of(tile * 256, 256), 256)
        total = jnp.zeros((TOK, 256), F32)
        for p in range(3):
            total = total + lax.dot_general(raw_ref[p], wbuf[p, at, :], NT, preferred_element_type=F32)
        ipart[:, at] = total
        return carry

    for p in range(3):
        pltpu.make_async_copy(w_ref.at[p], wbuf.at[p], w_sem.at[p]).wait()
    lax.fori_loop(0, D // 256, input_part, 0)
    isend[...] = ipart[...].astype(BF16)

    def input_copy(step):
        mate = lax.rem(head + step, 4)
        return pltpu.make_async_remote_copy(
            src_ref=isend.at[pl.ds(pl.multiple_of(mate * 32, 32), 32)], dst_ref=irecv.at[step],
            send_sem=i_ssem.at[step], recv_sem=i_rsem.at[step], device_id=(ctx, mate), device_id_type=MESH,
        )

    for step in range(1, 4):
        input_copy(step).start()

    def hand_on(p):
        gather(p, 0).wait_recv()
        gather(p, 2).start()
        gather(p, 5).start()
        gather(p, 1).wait_recv()
        gather(p, 3).start()
        gather(p, 6).start()

    def part_copy(p, step):
        mate = lax.rem(row + step, ROWS)
        return pltpu.make_async_remote_copy(
            src_ref=psend.at[p, pl.ds(pl.multiple_of(mate * PADDED, PADDED), PADDED)],
            dst_ref=precv.at[p, step], send_sem=p_ssem.at[p, step], recv_sem=p_rsem.at[p, step],
            device_id=(mate * ROW + col, head), device_id_type=MESH,
        )

    def finish(p):
        gather(p, 2).wait_recv()
        gather(p, 3).wait_recv()
        gather(p, 7).start()
        for kind in (4, 5, 6, 7):
            gather(p, kind).wait_recv()
        own(p).wait()

        def product(tile, carry):
            at = pl.ds(pl.multiple_of(tile * 256, 256), 256)
            made = jnp.dot(ht_ref[...], raws[p, :, at], preferred_element_type=F32)
            psend[p, :, at] = made.astype(BF16)
            part[:, at] = made
            return carry

        lax.fori_loop(0, wide // 256, product, 0)
        for step in range(1, ROWS):
            part_copy(p, step).start()
        wg_ref[p] = part[pl.ds(pl.multiple_of(row * PADDED, 8), SLAB), :]

    def receive(p):
        total = wg_ref[p]
        for step in range(1, ROWS):
            part_copy(p, step).wait_recv()
            total = total + precv[p, step].astype(F32)[:SLAB]
        wg_ref[p] = total

    hand_on(0)
    hand_on(1)
    finish(0)
    hand_on(2)
    finish(1)
    for step in range(1, 4):
        input_copy(step).wait_recv()
    total = ipart[pl.ds(pl.multiple_of(head * 32, 32), 32), :]
    for step in range(1, 4):
        total = total + irecv[step].astype(F32)
    ig_ref[...] = total.astype(BF16)
    finish(2)
    for p in range(3):
        receive(p)
    for p in range(3):
        for kind in range(8):
            gather(p, kind).wait_send()
        for step in range(1, ROWS):
            part_copy(p, step).wait_send()
    for step in range(1, 4):
        input_copy(step).wait_send()


def grads(raw, ht, proj_weight):
    vm = pl.BlockSpec(memory_space=pltpu.VMEM)
    dma = pltpu.SemaphoreType.DMA
    wide = HEADS * DK
    return pl.pallas_call(
        grads_kernel,
        out_shape=(
            jax.ShapeDtypeStruct((3, SLAB, wide), F32),
            jax.ShapeDtypeStruct((32, D), BF16),
        ),
        in_specs=[vm, vm, pl.BlockSpec(memory_space=pl.ANY)],
        out_specs=(vm, vm),
        scratch_shapes=[
            pltpu.VMEM((3, D, wide), BF16),
            pltpu.VMEM((3, ROW * TOK, wide), BF16),
            pltpu.VMEM((ROWS * PADDED, wide), F32),
            pltpu.VMEM((3, ROWS * PADDED, wide), BF16),
            pltpu.VMEM((3, ROWS, PADDED, wide), BF16),
            pltpu.VMEM((TOK, D), F32),
            pltpu.VMEM((TOK, D), BF16),
            pltpu.VMEM((4, 32, D), BF16),
            dma((3,)), dma((3,)), dma((3, 8)), dma((3, 8)), dma((3, ROWS)), dma((3, ROWS)), dma((4,)), dma((4,)),
        ],
        compiler_params=pltpu.CompilerParams(
            collective_id=1, has_side_effects=True, vmem_limit_bytes=56 * 1024 * 1024
        ),
        cost_estimate=pl.CostEstimate(flops=4_000_000_000, bytes_accessed=18_000_000, transcendentals=0),
        name="grads",
    )(raw, ht, proj_weight)


def body(hidden, proj_weight, conv_weight, log_decay, write_beta, saved_state, output_grad, doc_lengths):
    raw, decay_grad, ht = chain(
        doc_lengths, hidden, proj_weight, conv_weight, log_decay, write_beta, saved_state, output_grad
    )
    weight_grads, input_grad = grads(raw, ht, proj_weight)
    return (jnp.transpose(weight_grads, (1, 0, 2)), input_grad, decay_grad)


def solution(mesh):
    return jax.shard_map(
        body,
        mesh=mesh,
        in_specs=(
            P("ctx", None),
            P(None, None, "head"),
            P(None, None, "head"),
            P("ctx", "head"),
            P("ctx", "head"),
            P("ctx", "head", None, None),
            P("ctx", "head"),
            P(),
        ),
        out_specs=(P("ctx", None, "head"), P(("ctx", "head"), None), P("ctx", "head")),
        check_vma=False,
    )
```

```python
import functools

import jax
import jax.numpy as jnp
from jax import lax
from jax.experimental import pallas as pl
from jax.experimental.pallas import tpu as pltpu
from jax.sharding import PartitionSpec as P

MESH = pl.DeviceIdType.MESH
F32, BF16 = jnp.float32, jnp.bfloat16
EPSILON = 1e-06
HEADS, TOK, DK, D = 8, 128, 128, 2304
ROW, ROWS = 8, 4
SLAB, PADDED = 72, 80
HALO = 16
NN, NT, TN = (((1,), (0,)), ((), ())), (((1,), (1,)), ((), ())), (((0,), (0,)), ((), ()))


def dot1(a, b, form=NN):
    return lax.dot_general(a.astype(BF16), b.astype(BF16), form, preferred_element_type=F32)


def split(a):
    high = a.astype(BF16)
    return high, (a - high.astype(F32)).astype(BF16)


def dot3(a, b, form=NN):
    (ah, al), (bh, bl) = split(a), split(b)
    (la,), (lb,) = form[0]
    left = jnp.concatenate([ah, al, ah], axis=la)
    right = jnp.concatenate([bh, bh, bl], axis=lb)
    return lax.dot_general(left, right, form, preferred_element_type=F32)


def dot_exact_left(a, b):
    bh, bl = split(b)
    return lax.dot_general(
        jnp.concatenate([a, a], axis=1), jnp.concatenate([bh, bl], axis=0), NN, preferred_element_type=F32
    )


def iota(dim):
    return lax.broadcasted_iota(jnp.int32, (TOK, TOK), dim)


def me():
    return lax.axis_index("ctx"), lax.axis_index("head")


UNITS = ((0, 0, 512, 0), (0, 512, 512, 1), (1, 0, 512, 0), (2, 0, 512, 1), (1, 512, 512, 0), (2, 512, 512, 1))


def chain_kernel(
    doc_ref, hid_ref, w_ref, conv_ref, ld_hbm, beta_ref, s0_hbm, og_hbm,
    wg_ref, ig_ref, dld_ref,
    ld_ref, s0_ref, og_ref, xext, wbuf, pe, ht_t, ht_send, ht_recv, norm, val, inv, dsil, masks, bet,
    grow, shrink, edges, tinv, read, mb, rx, pc, tot, ry, carry_in, ds, rd, uu, wl, tk, dkm, gg,
    tail, spill, spill_in, own, raws, part, psend, precv, ipart, isend, irecv,
    in_sem, w_sem, x_sem, halo_sem, ht_ssem, ht_rsem, mb_ssem, mb_rsem, ry_ssem, ry_rsem, ds_ssem, ds_rsem, sp_sem,
    a_ssem, a_rsem, p_ssem, p_rsem, i_ssem, i_rsem,
):
    ctx, head = me()
    row, col = ctx // ROW, lax.rem(ctx, ROW)
    z, core = col // 2, lax.rem(col, 2)
    place = row * 2 + core
    after, before = lax.rem(ctx + 1, ROW * ROWS), lax.rem(ctx + ROW * ROWS - 1, ROW * ROWS)

    def w_copy(group):
        at = pl.ds(pl.multiple_of(group * 256, 256), 256)
        return pltpu.make_async_copy(w_ref.at[:, :, at], wbuf.at[:, :, at], w_sem.at[group])

    late = [
        pltpu.make_async_copy(src, dst, in_sem.at[k])
        for k, (src, dst) in enumerate(((ld_hbm, ld_ref), (og_hbm, og_ref), (s0_hbm, s0_ref)))
    ]
    late[0].start()
    for group in range(4):
        w_copy(group).start()
    for copy in late[1:]:
        copy.start()
    x_copy = pltpu.make_async_copy(hid_ref, xext.at[pl.ds(HALO, TOK)], x_sem)
    x_copy.start()

    barrier = pltpu.get_barrier_semaphore()
    for step in range(1, ROW):
        mate = row * ROW + lax.rem(col + step, ROW)
        pl.semaphore_signal(barrier, inc=1, device_id=(mate, head), device_id_type=MESH)
    for step in range(1, ROW):
        mate = lax.rem(place + step, ROW)
        mate = mate // 2 * ROW + z * 2 + lax.rem(mate, 2)
        pl.semaphore_signal(barrier, inc=1, device_id=(mate, head), device_id_type=MESH)
    for step in range(1, 4):
        pl.semaphore_signal(barrier, inc=1, device_id=(ctx, lax.rem(head + step, 4)), device_id_type=MESH)
    for mate in (after, before):
        pl.semaphore_signal(barrier, inc=1, device_id=(mate, head), device_id_type=MESH)

    t, s = iota(0), iota(1)
    first = ctx * TOK
    seg_t, seg_s = jnp.zeros_like(t), jnp.zeros_like(s)
    seg_last, start = jnp.int32(0), jnp.int32(0)
    for doc in range(8):
        seg_t = jnp.where(t + first >= start, jnp.maximum(seg_t, start), seg_t)
        seg_s = jnp.where(s + first >= start, jnp.maximum(seg_s, start), seg_s)
        seg_last = jnp.where(first + TOK - 1 >= start, jnp.maximum(seg_last, start), seg_last)
        start = start + doc_ref[doc]
    same = seg_t == seg_s
    masks[0] = jnp.where(same & (t > s), 1.0, 0.0)
    masks[1] = jnp.where(same & (t >= s), 1.0, 0.0)
    masks[2] = jnp.where(seg_t < first, 1.0, 0.0)
    masks[3] = jnp.where(seg_t == seg_last, 1.0, 0.0)
    for offset in range(1, 4):
        masks[3 + offset] = jnp.where(t + first - offset >= seg_t, 1.0, 0.0)
    lead_last = jnp.where(seg_last < first, 1.0, 0.0)
    for h in range(HEADS):
        bet[h] = jnp.broadcast_to(beta_ref[h : h + 1, :], (TOK, TOK)).T

    pl.semaphore_wait(barrier, 2 * (ROW - 1) + 3 + 2)

    halo = pltpu.make_async_remote_copy(
        src_ref=hid_ref.at[pl.ds(TOK - HALO, HALO)], dst_ref=xext.at[pl.ds(0, HALO)],
        send_sem=halo_sem.at[0], recv_sem=halo_sem.at[1], device_id=(after, head), device_id_type=MESH,
    )
    halo.start()

    for tile in range(D // 128):
        ht_t[tile * 128 : tile * 128 + 128] = hid_ref[:, tile * 128 : tile * 128 + 128].astype(F32).T
    ht_t[D : D + 8] = jnp.zeros((8, TOK), F32)
    for axis in range(2):
        for owner in range(ROW):
            for piece in range(ROWS):
                slab = (piece * ROW + owner, owner // 2 * ROW + piece * 2 + owner % 2)[axis]
                rows = slice(slab * SLAB, slab * SLAB + PADDED)
                ht_send[axis, owner, piece * PADDED : piece * PADDED + PADDED] = ht_t[rows].astype(BF16)
    spot = (col, place)

    def tokens(j):
        return pl.ds(pl.multiple_of(j * TOK, TOK), TOK)

    def ht_copy(axis, step):
        mate = lax.rem(spot[axis] + step, ROW)
        device = (row * ROW + mate, mate // 2 * ROW + z * 2 + lax.rem(mate, 2))[axis]
        return pltpu.make_async_remote_copy(
            src_ref=ht_send.at[axis, mate], dst_ref=ht_recv.at[axis, :, tokens(spot[axis])],
            send_sem=ht_ssem.at[axis, step], recv_sem=ht_rsem.at[axis, step],
            device_id=(device, head), device_id_type=MESH,
        )

    for step in range(1, ROW):
        for axis in range(2):
            ht_copy(axis, step).start()
    for axis in range(2):
        ht_recv[axis, :, tokens(spot[axis])] = ht_send[axis, spot[axis]]

    below = (iota(0) >= iota(1)).astype(F32).astype(BF16)
    late[0].wait()
    for h in range(HEADS):
        summed = dot_exact_left(below, ld_ref[:, h * DK : h * DK + DK])
        mid = summed[63:64]
        grow[h], shrink[h] = jnp.exp(summed - mid), jnp.exp(mid - summed)
        edges[h, 0:1], edges[h, 1:2] = jnp.exp(mid), jnp.exp(summed[TOK - 1 :] - mid)

    x_copy.wait()
    halo.wait()

    def project(group, carry):
        w_copy(group).wait()
        wide = pl.ds(pl.multiple_of(group * 256, 256), 256)
        for p in range(3):
            made = jnp.dot(xext[...], wbuf[p, :, wide], preferred_element_type=F32)
            pe[p, :, wide] = made.astype(BF16).astype(F32)
        for half in range(2):
            h = group * 2 + half
            lanes = pl.ds(pl.multiple_of(h * DK, DK), DK)
            for p in range(3):
                mixed = pe[p, pl.ds(HALO, TOK), lanes] * conv_ref[p, 0:1, lanes]
                for offset in range(1, 4):
                    tap = pe[p, pl.ds(HALO - offset, TOK), lanes] * conv_ref[p, offset : offset + 1, lanes]
                    mixed = mixed + tap * masks[3 + offset]
                gate = 1.0 / (1.0 + jnp.exp(-mixed))
                active = mixed * gate
                dsil[p, h] = gate * (1.0 + mixed * (1.0 - gate))
                if p == 2:
                    val[h] = active
                else:
                    scale = lax.rsqrt(jnp.sum(active * active, axis=1, keepdims=True) + EPSILON)
                    norm[p, h] = active * scale
                    inv[p, h] = jnp.broadcast_to(scale, (TOK, DK))
        return carry

    lax.fori_loop(0, 4, project, 0)

    def mb_copy(h):
        return pltpu.make_async_remote_copy(
            src_ref=mb.at[h], dst_ref=rx.at[col], send_sem=mb_ssem.at[h], recv_sem=mb_rsem.at[col],
            device_id=(row * ROW + h, head), device_id_type=MESH,
        )

    batch = 8

    def transition(step, carry):
        heads = [step * batch + k for k in range(batch)]
        lanes = [pl.ds(pl.multiple_of(h * DK, DK), DK) for h in heads]
        ups, downs = [grow[h] for h in heads], [shrink[h] for h in heads]
        firsts, lasts = [edges[h, 0:1] for h in heads], [edges[h, 1:2] for h in heads]
        betas = [bet[h] for h in heads]
        grads_out = [og_ref[:, lane] for lane in lanes]
        keys = [norm[1, h] for h in heads]
        queries = [norm[0, h] * DK ** (-0.5) for h in heads]
        low = [k * x for k, x in zip(keys, downs)]
        high = [jnp.concatenate([k * x, q * x], axis=0) for k, q, x in zip(keys, queries, ups)]
        both = [dot3(a, b, NT) for a, b in zip(high, low)]
        ns = [jnp.where(masks[0] > 0, x[:TOK], 0.0) * b for x, b in zip(both, betas)]
        rs = [jnp.where(masks[1] > 0, x[TOK:], 0.0) for x in both]
        apart = iota(0) ^ iota(1)
        eye = (apart == 0).astype(F32)
        solved = [eye - jnp.where(apart == 1, n, 0.0) for n in ns]
        for level in range(1, 7):
            edge = [jnp.where((apart >> level) == 1, n, 0.0) for n in ns]
            edge = [dot3(e, x) for e, x in zip(edge, solved)]
            solved = [x - dot3(x, e) for e, x in zip(edge, solved)]
        lead = masks[2]
        ups0 = [x * e * lead for x, e in zip(ups, firsts)]
        ws = [dot1(x, b * k * up) for x, b, k, up in zip(solved, betas, keys, ups0)]
        xs = [q * up - dot1(r, w) for q, up, r, w in zip(queries, ups0, rs, ws)]
        ends = [x * last * masks[3] for x, last in zip(low, lasts)]
        moves = [
            (eye * (last * e * lead_last) - dot1(w, end, TN)).astype(BF16)
            for w, end, last, e in zip(ws, ends, lasts, firsts)
        ]
        owns = [dot1(x, og, TN).astype(BF16) for x, og in zip(xs, grads_out)]
        backs = [dot1(x, end, TN).astype(BF16) for x, end in zip(solved, ends)]
        for h, move, own, back, x, r in zip(heads, moves, owns, backs, solved, rs):
            mb[h, :, 0:DK], mb[h, :, DK:] = move, own
            tk[h], tinv[h], read[h] = back, x, r.astype(BF16)
        for h in heads:
            @pl.when(h != col)
            def _():
                mb_copy(h).start()
        return carry

    for copy in late[1:]:
        copy.wait()
    lax.fori_loop(0, HEADS // batch, transition, 0)
    rx[col] = mb[col]

    def shift_back(p, lane, dmix):
        t = iota(0)
        main = dmix * conv_ref[p, 0:1, lane]
        over = jnp.zeros((TOK, DK), F32)
        for offset in range(1, 4):
            shifted = dmix * masks[3 + offset] * conv_ref[p, offset : offset + 1, lane]
            shifted = pltpu.roll(shifted, TOK - offset, 0)
            inside = t < TOK - offset
            main = main + jnp.where(inside, shifted, 0.0)
            over = over + jnp.where(inside, 0.0, shifted)
        return main, over

    def keep(p, lane, main, over):
        own[p, :, lane] = main.astype(BF16)
        tail[p, :, lane] = main[TOK - HALO :]
        spill[p, :, lane] = over[TOK - 8 :]

    def unnorm(n, scale, grad):
        return scale * (grad - n * jnp.sum(n * grad, axis=1, keepdims=True))

    def local(step, carry):
        heads = [step * 4 + k for k in range(4)]
        lanes = [pl.ds(pl.multiple_of(h * DK, DK), DK) for h in heads]
        ogs = [og_ref[:, lane] for lane in lanes]
        ups, downs = [grow[h] for h in heads], [shrink[h] for h in heads]
        ups0 = [up * edges[h, 0:1] * masks[2] for h, up in zip(heads, ups)]
        normed = [norm[0, h] for h in heads]
        qs = [n * DK ** (-0.5) for n in normed]
        ks = [norm[1, h] for h in heads]
        states = [s0_ref[0, h].astype(BF16) for h in heads]
        ts = [tinv[h].astype(BF16) for h in heads]
        slopes, scales = [dsil[0, h] for h in heads], [inv[0, h] for h in heads]
        recalled = [dot1(k * up, state) for k, up, state in zip(ks, ups0, states)]
        fed = [dot1(read[h], og, TN) for h, og in zip(heads, ogs)]
        crossed = [dot1(og, state, NT) for og, state in zip(ogs, states)]
        wanted = [bet[h] * (val[h] - x) for h, x in zip(heads, recalled)]
        us = [dot1(t, x).astype(BF16) for t, x in zip(ts, wanted)]
        wls = [dot1(t, x, TN) for t, x in zip(ts, fed)]
        dreads = [jnp.where(masks[1] > 0, dot1(og, u, NT), 0.0).astype(BF16) for og, u in zip(ogs, us)]
        dqs = [dot1(x, k * down) * up + y * up0 for x, k, down, up, y, up0 in zip(dreads, ks, downs, ups, crossed, ups0)]
        dkms = [dot1(x, q * up, TN) for x, q, up in zip(dreads, qs, ups)]
        ggs = [q * dq for q, dq in zip(qs, dqs)]
        dmix = [unnorm(n, scale, dq * DK ** (-0.5)) * slope for n, scale, dq, slope in zip(normed, scales, dqs, slopes)]
        raw = [shift_back(0, lane, x) for lane, x in zip(lanes, dmix)]
        for h, lane, u, wlocal, km, g, (main, over) in zip(heads, lanes, us, wls, dkms, ggs, raw):
            uu[h], wl[h], dkm[h], gg[h] = u, wlocal, km, g
            keep(0, lane, main, over)
        return carry

    def spill_copy(at):
        p, first, width = ((0, 0, 1024), (1, 0, 512), (1, 512, 512))[at]
        block = (pl.ds(p, min(p + 1, 2)), slice(None), pl.ds(first, width))
        return pltpu.make_async_remote_copy(
            src_ref=spill.at[block], dst_ref=spill_in.at[block], send_sem=sp_sem.at[at, 0],
            recv_sem=sp_sem.at[at, 1], device_id=(before, head), device_id_type=MESH,
        )

    def add_spill(p, first, width, axis):
        at = pl.ds(first, width)
        low = tail[p, 8:16, at] + spill_in[p, :, at]
        own[p, TOK - HALO :, at] = jnp.concatenate([tail[p, 0:8, at], low], axis=0).astype(BF16)
        raws[p, tokens(spot[axis]), at] = own[p, :, at]

    def along(axis, step, other=0):
        to = lax.rem(core + other, 2)
        if axis == 0:
            return (row * ROW + lax.rem(z + step, 4) * 2 + to, head)
        return (lax.rem(row + step, 4) * ROW + z * 2 + to, head)

    def gather(unit, kind):
        p, first, width, axis = UNITS[unit]
        off = (0, 0, 3, 1, 0, 3, 1, 2)[kind]
        if kind == 2:
            at = pl.ds(first, width // 2)
        elif kind == 3:
            at = pl.ds(first + width // 2, width // 2)
        else:
            at = pl.ds(first, width)
        slot = lax.rem((z, row)[axis] + off, 4) * 2 + core
        block = raws.at[p, tokens(slot), at]
        to = along(axis, (1, 3, 1, 3, 0, 0, 0, 0)[kind], kind // 4)
        return pltpu.make_async_remote_copy(
            src_ref=block, dst_ref=block, send_sem=a_ssem.at[unit, kind], recv_sem=a_rsem.at[unit, kind],
            device_id=to, device_id_type=MESH,
        )

    def set_out(unit):
        add_spill(*UNITS[unit])
        for kind in (0, 1, 4):
            gather(unit, kind).start()

    def hand_on(unit):
        gather(unit, 0).wait_recv()
        gather(unit, 2).start()
        gather(unit, 5).start()
        gather(unit, 1).wait_recv()
        gather(unit, 3).start()
        gather(unit, 6).start()

    def part_copy(unit, step):
        p, first, width, axis = UNITS[unit]
        mate = lax.rem((row, z)[axis] + step, ROWS)
        at = pl.ds(first, width)
        return pltpu.make_async_remote_copy(
            src_ref=psend.at[p, pl.ds(pl.multiple_of(mate * PADDED, PADDED), PADDED), at],
            dst_ref=precv.at[p, step, :, at], send_sem=p_ssem.at[unit, step], recv_sem=p_rsem.at[unit, step],
            device_id=along(1 - axis, step), device_id_type=MESH,
        )

    def finish(unit):
        p, first, width, axis = UNITS[unit]
        gather(unit, 2).wait_recv()
        gather(unit, 3).wait_recv()
        gather(unit, 7).start()
        for kind in (4, 5, 6, 7):
            gather(unit, kind).wait_recv()

        def product(tile, carry):
            at = pl.ds(pl.multiple_of(first + tile * 256, 256), 256)
            made = jnp.dot(ht_recv[axis], raws[p, :, at], preferred_element_type=F32)
            psend[p, :, at] = made.astype(BF16)
            part[:, at] = made
            return carry

        lax.fori_loop(0, width // 256, product, 0)
        for step in range(1, ROWS):
            part_copy(unit, step).start()
        at = pl.ds(first, width)
        wg_ref[p, :, at] = part[pl.ds(pl.multiple_of((row, z)[axis] * PADDED, 8), SLAB), at]

    def receive(unit):
        p, first, width, axis = UNITS[unit]
        at = pl.ds(first, width)
        total = wg_ref[p, :, at]
        for step in range(1, ROWS):
            part_copy(unit, step).wait_recv()
            total = total + precv[p, step, :, at].astype(F32)[:SLAB]
        wg_ref[p, :, at] = total

    def input_part(low, high):
        def one(tile, carry):
            at = pl.ds(pl.multiple_of(tile * 256, 256), 256)
            total = jnp.zeros((TOK, 256), F32) if low == 0 else ipart[:, at]
            for p in range(low, high):
                mine = own[p]
                total = total + lax.dot_general(mine, wbuf[p, at, :], NT, preferred_element_type=F32)
            ipart[:, at] = total
            if high == 3:
                isend[:, at] = total.astype(BF16)
            return carry

        lax.fori_loop(0, D // 256, one, 0)

    def input_copy(step):
        mate = lax.rem(head + step, 4)
        return pltpu.make_async_remote_copy(
            src_ref=isend.at[pl.ds(pl.multiple_of(mate * 32, 32), 32)], dst_ref=irecv.at[step],
            send_sem=i_ssem.at[step], recv_sem=i_rsem.at[step], device_id=(ctx, mate), device_id_type=MESH,
        )

    lax.fori_loop(0, HEADS // 4, local, 0)
    spill_copy(0).start()

    for j in range(ROW):
        @pl.when(j != col)
        def _():
            pltpu.make_async_remote_copy(
                src_ref=mb.at[j], dst_ref=rx.at[j], send_sem=mb_ssem.at[j], recv_sem=mb_rsem.at[j],
                device_id=(row * ROW + j, head), device_id_type=MESH,
            ).wait_recv()

    spill_copy(0).wait_recv()
    set_out(0)
    set_out(1)

    def compose(m, x, b):
        hi, lo = split(x)
        out = jnp.dot(m, jnp.concatenate([hi, lo], axis=1), preferred_element_type=F32)
        n = x.shape[1]
        return out[:, :n] + out[:, n:] + b

    half = ROW // 2
    zeros = jnp.zeros((DK, DK), F32)
    ends = [rx[half - 1].astype(F32), rx[ROW - 1].astype(F32)]
    for j in range(half - 2, -1, -1):
        for k in range(2):
            at = k * half + j
            pc[at] = ends[k]
            b = jnp.concatenate([zeros, rx[at, :, DK:].astype(F32)], axis=1)
            ends[k] = compose(rx[at, :, 0:DK], ends[k], b)
    b = jnp.concatenate([zeros, ends[0][:, DK:]], axis=1)
    tot[...] = (dot3(ends[0][:, 0:DK], ends[1]) + b).astype(BF16)

    def ry_copy(step):
        mate = lax.rem(row + step, ROWS) * ROW + col
        return pltpu.make_async_remote_copy(
            src_ref=tot, dst_ref=ry.at[ROWS - step], send_sem=ry_ssem.at[step], recv_sem=ry_rsem.at[step],
            device_id=(mate, head), device_id_type=MESH,
        )

    for step in range(1, ROWS):
        @pl.when(row + step >= ROWS)
        def _():
            ry_copy(step).start()

    hand_on(0)
    hand_on(1)
    for axis in range(2):
        for step in range(1, ROW):
            ht_copy(axis, step).wait()
    carry_in[...] = zeros
    for k in range(ROWS - 1, 0, -1):
        @pl.when(row + k < ROWS)
        def _():
            ry_copy(ROWS - k).wait_recv()
            carry_in[...] = compose(ry[k, :, 0:DK], carry_in[...], ry[k, :, DK:].astype(F32))

    total = carry_in[...]

    def ds_copy(j):
        return pltpu.make_async_remote_copy(
            src_ref=ds.at[j], dst_ref=rd.at[col], send_sem=ds_ssem.at[j], recv_sem=ds_rsem.at[col],
            device_id=(row * ROW + j, head), device_id_type=MESH,
        )

    middle = dot3(ends[1][:, 0:DK], total) + ends[1][:, DK:]
    entries = [middle.astype(BF16), total.astype(BF16)]
    for j in range(ROW):
        if j % half == half - 1:
            ds[j] = entries[j // half]
        else:
            ds[j] = (dot1(pc[j, :, 0:DK], entries[j // half]) + pc[j, :, DK:]).astype(BF16)

        @pl.when(j != col)
        def _():
            ds_copy(j).start()

    rd[col] = ds[col]

    finish(0)
    finish(1)
    input_part(0, 1)

    for j in range(ROW):
        @pl.when(j != col)
        def _():
            pltpu.make_async_remote_copy(
                src_ref=ds.at[j], dst_ref=rd.at[j], send_sem=ds_ssem.at[j], recv_sem=ds_rsem.at[j],
                device_id=(row * ROW + j, head), device_id_type=MESH,
            ).wait_recv()

    def carried(step, carry):
        heads = [step * 4 + k for k in range(4)]
        lanes = [pl.ds(pl.multiple_of(h * DK, DK), DK) for h in heads]
        above = (iota(1) >= iota(0)).astype(F32).astype(BF16)
        ones = jnp.ones((8, DK), BF16)
        lead = masks[2]
        ups, downs = [grow[h] for h in heads], [shrink[h] for h in heads]
        firsts, lasts = [edges[h, 0:1] for h in heads], [edges[h, 1:2] for h in heads]
        ks = [norm[1, h] for h in heads]
        nexts = [rd[h] for h in heads]
        states = [s0_ref[0, h] for h in heads]
        us = [uu[h] for h in heads]
        read_dkm, read_gg = [dkm[h] for h in heads], [gg[h] for h in heads]
        slopes = [(dsil[1, h], dsil[2, h]) for h in heads]
        scales = [inv[1, h] for h in heads]
        bws = [bet[h] * (wl[h] + dot1(tk[h], x)) for h, x in zip(heads, nexts)]
        das = [jnp.where(masks[0] > 0, -dot1(bw, u, NT), 0.0).astype(BF16) for bw, u in zip(bws, us)]
        olds = [dot1(bw * lead, state, NT) * e for bw, state, e in zip(bws, states, firsts)]
        dkus = [dot1(da, k * down) - old for da, k, down, old in zip(das, ks, downs, olds)]
        dkms = [x + dot1(da, k * up, TN) for x, da, k, up in zip(read_dkm, das, ks, ups)]
        dends = [dot1(u, x, NT) * e * masks[3] for u, x, e in zip(us, nexts, lasts)]
        risings = [x * up for x, up in zip(dkus, ups)]
        endings = [x * down for x, down in zip(dends, downs)]
        fallings = [x * down + y for x, down, y in zip(dkms, downs, endings)]
        dmix = [
            unnorm(k, scale, x + y) * slope[0]
            for k, scale, x, y, slope in zip(ks, scales, risings, fallings, slopes)
        ]
        raw1 = [shift_back(1, lane, x) for lane, x in zip(lanes, dmix)]
        raw2 = [shift_back(2, lane, bw * slope[1]) for lane, bw, slope in zip(lanes, bws, slopes)]
        for lane, one, two in zip(lanes, raw1, raw2):
            keep(1, lane, *one)
            keep(2, lane, *two)
        dgs = [g + k * (x - y) for g, k, x, y in zip(read_gg, ks, risings, fallings)]
        crossed = [split(state * x.astype(F32) * lead_last) for state, x in zip(states, nexts)]
        extras = [dot1(ones, ch, NT) + dot1(ones, cl, NT) for ch, cl in crossed]
        extras = [
            x[0:1] * e * last + jnp.sum(k * y, axis=0, keepdims=True)
            for x, e, last, k, y in zip(extras, firsts, lasts, ks, endings)
        ]
        dlds = [dot_exact_left(above, dg) + x for dg, x in zip(dgs, extras)]
        for lane, x in zip(lanes, dlds):
            dld_ref[:, lane] = x
        return carry

    carried(0, 0)
    spill_copy(1).start()
    carried(1, 0)
    spill_copy(2).start()
    spill_copy(1).wait_recv()
    set_out(2)
    set_out(3)
    spill_copy(2).wait_recv()
    set_out(4)
    set_out(5)
    hand_on(2)
    hand_on(3)
    input_part(1, 3)
    for step in range(1, 4):
        input_copy(step).start()
    finish(2)
    finish(3)
    hand_on(4)
    hand_on(5)
    receive(0)
    receive(1)
    finish(4)
    finish(5)
    for step in range(1, 4):
        input_copy(step).wait_recv()
    total = ipart[pl.ds(pl.multiple_of(head * 32, 32), 32), :]
    for step in range(1, 4):
        total = total + irecv[step].astype(F32)
    ig_ref[...] = total.astype(BF16)
    for unit in range(2, len(UNITS)):
        receive(unit)

    for at in range(3):
        spill_copy(at).wait_send()
    for step in range(1, ROWS):
        input_copy(step).wait_send()

        @pl.when(row + step >= ROWS)
        def _():
            ry_copy(step).wait_send()

    for j in range(ROW):
        @pl.when(j != col)
        def _():
            mb_copy(j).wait_send()
            ds_copy(j).wait_send()
    for unit in range(len(UNITS)):
        for kind in range(8):
            gather(unit, kind).wait_send()
        for step in range(1, ROWS):
            part_copy(unit, step).wait_send()


def chain(doc_lengths, hidden, proj_weight, conv_weight, log_decay, write_beta, saved_state, output_grad):
    vm = pl.BlockSpec(memory_space=pltpu.VMEM)
    hbm = pl.BlockSpec(memory_space=pl.ANY)
    sq = (HEADS, TOK, DK)
    dma = pltpu.SemaphoreType.DMA
    return pl.pallas_call(
        chain_kernel,
        out_shape=(
            jax.ShapeDtypeStruct((3, SLAB, HEADS * DK), F32),
            jax.ShapeDtypeStruct((32, D), BF16),
            jax.ShapeDtypeStruct((TOK, HEADS * DK), F32),
        ),
        in_specs=[pl.BlockSpec(memory_space=pltpu.SMEM), vm, hbm, vm, hbm, vm, hbm, hbm],
        out_specs=(vm, vm, vm),
        scratch_shapes=[
            pltpu.VMEM((TOK, HEADS * DK), F32),
            pltpu.VMEM((1,) + sq, F32),
            pltpu.VMEM((TOK, HEADS * DK), BF16),
            pltpu.VMEM((HALO + TOK, D), BF16),
            pltpu.VMEM((3, D, HEADS * DK), BF16),
            pltpu.VMEM((3, HALO + TOK, HEADS * DK), F32),
            pltpu.VMEM((D + 8, TOK), F32),
            pltpu.VMEM((2, ROW, ROWS * PADDED, TOK), BF16),
            pltpu.VMEM((2, ROWS * PADDED, ROW * TOK), BF16),
            pltpu.VMEM((2,) + sq, F32),
            pltpu.VMEM(sq, F32),
            pltpu.VMEM((2,) + sq, F32),
            pltpu.VMEM((3,) + sq, F32),
            pltpu.VMEM((7, TOK, TOK), F32),
            pltpu.VMEM(sq, F32),
            pltpu.VMEM(sq, F32),
            pltpu.VMEM(sq, F32),
            pltpu.VMEM((HEADS, 8, DK), F32),
            pltpu.VMEM(sq, F32),
            pltpu.VMEM(sq, BF16),
            pltpu.VMEM((HEADS, DK, 2 * DK), BF16),
            pltpu.VMEM((ROW, DK, 2 * DK), BF16),
            pltpu.VMEM((ROW, DK, 2 * DK), F32),
            pltpu.VMEM((DK, 2 * DK), BF16),
            pltpu.VMEM((ROWS, DK, 2 * DK), BF16),
            pltpu.VMEM((DK, DK), F32),
            pltpu.VMEM((ROW, DK, DK), BF16),
            pltpu.VMEM((HEADS, DK, DK), BF16),
            pltpu.VMEM(sq, BF16),
            pltpu.VMEM(sq, F32),
            pltpu.VMEM(sq, BF16),
            pltpu.VMEM(sq, F32),
            pltpu.VMEM(sq, F32),
            pltpu.VMEM((3, HALO, HEADS * DK), F32),
            pltpu.VMEM((3, 8, HEADS * DK), F32),
            pltpu.VMEM((3, 8, HEADS * DK), F32),
            pltpu.VMEM((3, TOK, HEADS * DK), BF16),
            pltpu.VMEM((3, ROW * TOK, HEADS * DK), BF16),
            pltpu.VMEM((ROWS * PADDED, HEADS * DK), F32),
            pltpu.VMEM((3, ROWS * PADDED, HEADS * DK), BF16),
            pltpu.VMEM((3, ROWS, PADDED, HEADS * DK), BF16),
            pltpu.VMEM((TOK, D), F32),
            pltpu.VMEM((TOK, D), BF16),
            pltpu.VMEM((4, 32, D), BF16),
            dma((3,)), dma((4,)), dma, dma((2,)), dma((2, ROW)), dma((2, ROW)), dma((ROW,)), dma((ROW,)),
            dma((ROWS,)), dma((ROWS,)), dma((ROW,)), dma((ROW,)), dma((3, 2)),
            dma((len(UNITS), 8)), dma((len(UNITS), 8)), dma((len(UNITS), ROWS)), dma((len(UNITS), ROWS)), dma((4,)), dma((4,)),
        ],
        compiler_params=pltpu.CompilerParams(
            collective_id=0, has_side_effects=True, vmem_limit_bytes=56 * 1024 * 1024
        ),
        cost_estimate=pl.CostEstimate(flops=8_000_000_000, bytes_accessed=18_000_000, transcendentals=1_000_000),
        name="chain",
    )(doc_lengths, hidden, proj_weight, conv_weight, log_decay, write_beta.T, saved_state, output_grad)


def settle_kernel(wg_ref, ig_ref, dld_ref, wg_out, ig_out, dld_out, wg, ig, dld, sems):
    moves = ((wg_ref, wg, wg_out), (dld_ref, dld, dld_out), (ig_ref, ig, ig_out))
    inward = [pltpu.make_async_copy(src, mid, sems.at[0, k]) for k, (src, mid, dst) in enumerate(moves)]
    outward = [pltpu.make_async_copy(mid, dst, sems.at[1, k]) for k, (src, mid, dst) in enumerate(moves)]
    for copy in inward:
        copy.start()
    for arrived, copy in zip(inward, outward):
        arrived.wait()
        copy.start()
    for copy in outward:
        copy.wait()


def settle(*arrays):
    anywhere = pl.BlockSpec(memory_space=pl.ANY)
    return pl.pallas_call(
        settle_kernel,
        out_shape=tuple(jax.ShapeDtypeStruct(a.shape, a.dtype) for a in arrays),
        in_specs=[anywhere] * 3,
        out_specs=(anywhere,) * 3,
        scratch_shapes=[pltpu.VMEM(a.shape, a.dtype) for a in arrays] + [pltpu.SemaphoreType.DMA((2, 3))],
        name="settle",
    )(*arrays)


def body(hidden, proj_weight, conv_weight, log_decay, write_beta, saved_state, output_grad, doc_lengths):
    weight_grads, input_grad, decay_grad = settle(
        *chain(doc_lengths, hidden, proj_weight, conv_weight, log_decay, write_beta, saved_state, output_grad)
    )
    return (jnp.transpose(weight_grads, (1, 0, 2)), input_grad, decay_grad)


def solution(mesh):
    return jax.shard_map(
        body,
        mesh=mesh,
        in_specs=(
            P("ctx", None),
            P(None, None, "head"),
            P(None, None, "head"),
            P("ctx", "head"),
            P("ctx", "head"),
            P("ctx", "head", None, None),
            P("ctx", "head"),
            P(),
        ),
        out_specs=(P("ctx", None, "head"), P(("ctx", "head"), None), P("ctx", "head")),
        check_vma=False,
    )
```

```python
import functools

import jax
import jax.numpy as jnp
from jax import lax
from jax.experimental import pallas as pl
from jax.experimental.pallas import tpu as pltpu
from jax.sharding import PartitionSpec as P

MESH = pl.DeviceIdType.MESH
F32, BF16 = jnp.float32, jnp.bfloat16
EPSILON = 1e-06
HEADS, TOK, DK, D = 8, 128, 128, 2304
ROW, ROWS = 8, 4
SLAB, HALF = 72, 256
HALO = 16
NN, NT, TN = (((1,), (0,)), ((), ())), (((1,), (1,)), ((), ())), (((0,), (0,)), ((), ()))


def dot1(a, b, form=NN):
    return lax.dot_general(a.astype(BF16), b.astype(BF16), form, preferred_element_type=F32)


def split(a):
    high = a.astype(BF16)
    return high, (a - high.astype(F32)).astype(BF16)


def dot3(a, b, form=NN):
    (ah, al), (bh, bl) = split(a), split(b)
    (la,), (lb,) = form[0]
    left = jnp.concatenate([ah, al, ah], axis=la)
    right = jnp.concatenate([bh, bh, bl], axis=lb)
    return lax.dot_general(left, right, form, preferred_element_type=F32)


def two_pass(a, b):
    ah, al = split(a)
    return lax.dot_general(
        jnp.concatenate([ah, al], axis=1), jnp.concatenate([b, b], axis=0), NN, preferred_element_type=F32
    )


def dot_exact_left(a, b):
    bh, bl = split(b)
    return lax.dot_general(
        jnp.concatenate([a, a], axis=1), jnp.concatenate([bh, bl], axis=0), NN, preferred_element_type=F32
    )


def iota(dim):
    return lax.broadcasted_iota(jnp.int32, (TOK, TOK), dim)


def me():
    return lax.axis_index("ctx"), lax.axis_index("head")


UNITS = ((0, 0, 512, 0), (0, 512, 512, 1), (1, 0, 512, 0), (2, 0, 512, 1), (1, 512, 512, 0), (2, 512, 512, 1))
FAR_FIRST = (4, 5, 3, 2, 6, 7, 1)


def chain_kernel(
    doc_ref, hid_ref, w_ref, conv_ref, ld_hbm, beta_ref, s0_hbm, og_hbm,
    wg_ref, ig_ref, dld_ref,
    ld_ref, s0_ref, og_ref, xext, wbuf, pe, ht_t, ht_send, ht_recv, norm, val, inv, dsil, masks, bet,
    grow, shrink, edges, tinv, read, mb, rx, pc, tot, ry, carry_in, ds, rd, uu, wl, tk, dkm, gg,
    tail, spill, spill_in, own, raws, part, psend, precv, ipart, isend, irecv,
    in_sem, w_sem, x_sem, halo_sem, ht_ssem, ht_rsem, mb_ssem, mb_rsem, ry_ssem, ry_rsem, ds_ssem, ds_rsem, sp_sem,
    a_ssem, a_rsem, p_ssem, p_rsem, i_ssem, i_rsem,
):
    ctx, head = me()
    row, col = ctx // ROW, lax.rem(ctx, ROW)
    z, core = col // 2, lax.rem(col, 2)
    place = row * 2 + core
    after, before = lax.rem(ctx + 1, ROW * ROWS), lax.rem(ctx + ROW * ROWS - 1, ROW * ROWS)

    def w_copy(group):
        at = pl.ds(pl.multiple_of(group * 256, 256), 256)
        return pltpu.make_async_copy(w_ref.at[:, :, at], wbuf.at[:, :, at], w_sem.at[group])

    late = [
        pltpu.make_async_copy(src, dst, in_sem.at[k])
        for k, (src, dst) in enumerate(((ld_hbm, ld_ref), (og_hbm, og_ref), (s0_hbm, s0_ref)))
    ]
    late[0].start()
    for group in range(4):
        w_copy(group).start()
    for copy in late[1:]:
        copy.start()
    x_copy = pltpu.make_async_copy(hid_ref, xext.at[pl.ds(HALO, TOK)], x_sem)
    x_copy.start()

    barrier = pltpu.get_barrier_semaphore()
    for step in range(1, ROW):
        mate = row * ROW + lax.rem(col + step, ROW)
        pl.semaphore_signal(barrier, inc=1, device_id=(mate, head), device_id_type=MESH)
    for step in range(1, ROW):
        mate = lax.rem(place + step, ROW)
        mate = mate // 2 * ROW + z * 2 + lax.rem(mate, 2)
        pl.semaphore_signal(barrier, inc=1, device_id=(mate, head), device_id_type=MESH)
    for step in range(1, 4):
        pl.semaphore_signal(barrier, inc=1, device_id=(ctx, lax.rem(head + step, 4)), device_id_type=MESH)
    for mate in (after, before):
        pl.semaphore_signal(barrier, inc=1, device_id=(mate, head), device_id_type=MESH)

    t, s = iota(0), iota(1)
    first = ctx * TOK
    seg_t, seg_s = jnp.zeros_like(t), jnp.zeros_like(s)
    seg_last, start = jnp.int32(0), jnp.int32(0)
    for doc in range(8):
        seg_t = jnp.where(t + first >= start, jnp.maximum(seg_t, start), seg_t)
        seg_s = jnp.where(s + first >= start, jnp.maximum(seg_s, start), seg_s)
        seg_last = jnp.where(first + TOK - 1 >= start, jnp.maximum(seg_last, start), seg_last)
        start = start + doc_ref[doc]
    same = seg_t == seg_s
    masks[0] = jnp.where(same & (t > s), 1.0, 0.0)
    masks[1] = jnp.where(same & (t >= s), 1.0, 0.0)
    masks[2] = jnp.where(seg_t < first, 1.0, 0.0)
    masks[3] = jnp.where(seg_t == seg_last, 1.0, 0.0)
    for offset in range(1, 4):
        masks[3 + offset] = jnp.where(t + first - offset >= seg_t, 1.0, 0.0)
    lead_last = jnp.where(seg_last < first, 1.0, 0.0)
    for h in range(HEADS):
        bet[h] = jnp.broadcast_to(beta_ref[h : h + 1, :], (TOK, TOK)).T

    pl.semaphore_wait(barrier, 2 * (ROW - 1) + 3 + 2)

    halo = pltpu.make_async_remote_copy(
        src_ref=hid_ref.at[pl.ds(TOK - HALO, HALO)], dst_ref=xext.at[pl.ds(0, HALO)],
        send_sem=halo_sem.at[0], recv_sem=halo_sem.at[1], device_id=(after, head), device_id_type=MESH,
    )
    halo.start()

    for tile in range(D // 128):
        ht_t[tile * 128 : tile * 128 + 128] = hid_ref[:, tile * 128 : tile * 128 + 128].astype(F32).T
    for axis in range(2):
        for owner in range(ROW):
            slabs = [
                (piece * ROW + owner, owner // 2 * ROW + piece * 2 + owner % 2)[axis] for piece in range(ROWS)
            ]
            rows = [ht_t[slab * SLAB : slab * SLAB + SLAB] for slab in slabs]
            ht_send[axis, owner] = jnp.concatenate(rows, axis=0).astype(BF16)
    spot = (col, place)

    def tokens(j):
        return pl.ds(pl.multiple_of(j * TOK, TOK), TOK)

    def ht_copy(axis, step):
        mate = lax.rem(spot[axis] + step, ROW)
        device = (row * ROW + mate, mate // 2 * ROW + z * 2 + lax.rem(mate, 2))[axis]
        return pltpu.make_async_remote_copy(
            src_ref=ht_send.at[axis, mate], dst_ref=ht_recv.at[axis, :, tokens(spot[axis])],
            send_sem=ht_ssem.at[axis, step], recv_sem=ht_rsem.at[axis, step],
            device_id=(device, head), device_id_type=MESH,
        )

    for step in range(1, ROW):
        for axis in range(2):
            ht_copy(axis, step).start()
    for axis in range(2):
        ht_recv[axis, :, tokens(spot[axis])] = ht_send[axis, spot[axis]]

    below = (iota(0) >= iota(1)).astype(F32).astype(BF16)
    late[0].wait()
    for h in range(HEADS):
        summed = dot_exact_left(below, ld_ref[:, h * DK : h * DK + DK])
        mid = summed[63:64]
        grow[h], shrink[h] = jnp.exp(summed - mid), jnp.exp(mid - summed)
        edges[h, 0:1], edges[h, 1:2] = jnp.exp(mid), jnp.exp(summed[TOK - 1 :] - mid)

    x_copy.wait()
    halo.wait()

    def project(group, carry):
        w_copy(group).wait()
        wide = pl.ds(pl.multiple_of(group * 256, 256), 256)
        for p in range(3):
            made = jnp.dot(xext[...], wbuf[p, :, wide], preferred_element_type=F32)
            pe[p, :, wide] = made.astype(BF16).astype(F32)
        for half in range(2):
            h = group * 2 + half
            lanes = pl.ds(pl.multiple_of(h * DK, DK), DK)
            for p in range(3):
                mixed = pe[p, pl.ds(HALO, TOK), lanes] * conv_ref[p, 0:1, lanes]
                for offset in range(1, 4):
                    tap = pe[p, pl.ds(HALO - offset, TOK), lanes] * conv_ref[p, offset : offset + 1, lanes]
                    mixed = mixed + tap * masks[3 + offset]
                gate = 1.0 / (1.0 + jnp.exp(-mixed))
                active = mixed * gate
                dsil[p, h] = gate * (1.0 + mixed * (1.0 - gate))
                if p == 2:
                    val[h] = active
                else:
                    scale = lax.rsqrt(jnp.sum(active * active, axis=1, keepdims=True) + EPSILON)
                    norm[p, h] = active * scale
                    inv[p, h] = jnp.broadcast_to(scale, (TOK, DK))
        return carry

    lax.fori_loop(0, 4, project, 0)

    def mb_copy(h):
        return pltpu.make_async_remote_copy(
            src_ref=mb.at[h], dst_ref=rx.at[col], send_sem=mb_ssem.at[h], recv_sem=mb_rsem.at[col],
            device_id=(row * ROW + h, head), device_id_type=MESH,
        )

    batch = 8

    def transition(step, carry):
        heads = [step * batch + k for k in range(batch)]
        lanes = [pl.ds(pl.multiple_of(h * DK, DK), DK) for h in heads]
        ups, downs = [grow[h] for h in heads], [shrink[h] for h in heads]
        firsts, lasts = [edges[h, 0:1] for h in heads], [edges[h, 1:2] for h in heads]
        betas = [bet[h] for h in heads]
        grads_out = [og_ref[:, lane] for lane in lanes]
        keys = [norm[1, h] for h in heads]
        queries = [norm[0, h] * DK ** (-0.5) for h in heads]
        low = [k * x for k, x in zip(keys, downs)]
        high = [jnp.concatenate([k * x, q * x], axis=0) for k, q, x in zip(keys, queries, ups)]
        both = [dot3(a, b, NT) for a, b in zip(high, low)]
        ns = [jnp.where(masks[0] > 0, x[:TOK], 0.0) * b for x, b in zip(both, betas)]
        rs = [jnp.where(masks[1] > 0, x[TOK:], 0.0) for x in both]
        apart = iota(0) ^ iota(1)
        eye = (apart == 0).astype(F32)
        solved = [eye - jnp.where(apart == 1, n, 0.0) for n in ns]
        for level in range(1, 7):
            edge = [jnp.where((apart >> level) == 1, n, 0.0) for n in ns]
            edge = [dot3(e, x) for e, x in zip(edge, solved)]
            solved = [x - dot3(x, e) for e, x in zip(edge, solved)]
        lead = masks[2]
        ups0 = [x * e * lead for x, e in zip(ups, firsts)]
        ws = [dot3(x, b * k * up) for x, b, k, up in zip(solved, betas, keys, ups0)]
        xs = [q * up - dot1(r, w) for q, up, r, w in zip(queries, ups0, rs, ws)]
        ends = [x * last * masks[3] for x, last in zip(low, lasts)]
        moves = [
            (eye * (last * e * lead_last) - dot1(w, end, TN)).astype(BF16)
            for w, end, last, e in zip(ws, ends, lasts, firsts)
        ]
        owns = [dot1(x, og, TN).astype(BF16) for x, og in zip(xs, grads_out)]
        backs = [dot3(x, end, TN) for x, end in zip(solved, ends)]
        for h, move, own, back, x, r in zip(heads, moves, owns, backs, solved, rs):
            mb[h, :, 0:DK], mb[h, :, DK:] = move, own
            tk[h], tinv[h], read[h] = back, x, r.astype(BF16)
        for step in FAR_FIRST:
            mb_copy(lax.rem(col + step, ROW)).start()
        return carry

    for copy in late[1:]:
        copy.wait()
    lax.fori_loop(0, HEADS // batch, transition, 0)
    rx[col] = mb[col]

    def shift_back(p, lane, dmix):
        t = iota(0)
        main = dmix * conv_ref[p, 0:1, lane]
        over = jnp.zeros((TOK, DK), F32)
        for offset in range(1, 4):
            shifted = dmix * masks[3 + offset] * conv_ref[p, offset : offset + 1, lane]
            shifted = pltpu.roll(shifted, TOK - offset, 0)
            inside = t < TOK - offset
            main = main + jnp.where(inside, shifted, 0.0)
            over = over + jnp.where(inside, 0.0, shifted)
        return main, over

    def keep(p, lane, main, over):
        own[p, :, lane] = main.astype(BF16)
        tail[p, :, lane] = main[TOK - HALO :]
        spill[p, :, lane] = over[TOK - 8 :]

    def unnorm(n, scale, grad):
        return scale * (grad - n * jnp.sum(n * grad, axis=1, keepdims=True))

    def local(step, carry):
        heads = [step * 4 + k for k in range(4)]
        lanes = [pl.ds(pl.multiple_of(h * DK, DK), DK) for h in heads]
        ogs = [og_ref[:, lane] for lane in lanes]
        ups, downs = [grow[h] for h in heads], [shrink[h] for h in heads]
        ups0 = [up * edges[h, 0:1] * masks[2] for h, up in zip(heads, ups)]
        normed = [norm[0, h] for h in heads]
        qs = [n * DK ** (-0.5) for n in normed]
        ks = [norm[1, h] for h in heads]
        states = [s0_ref[0, h] for h in heads]
        ts = [tinv[h] for h in heads]
        slopes, scales = [dsil[0, h] for h in heads], [inv[0, h] for h in heads]
        recalled = [dot3(k * up, state) for k, up, state in zip(ks, ups0, states)]
        fed = [dot1(read[h], og, TN) for h, og in zip(heads, ogs)]
        crossed = [dot1(og, state, NT) for og, state in zip(ogs, states)]
        wanted = [bet[h] * (val[h] - x) for h, x in zip(heads, recalled)]
        us = [dot3(t, x).astype(BF16) for t, x in zip(ts, wanted)]
        wls = [dot3(t, x, TN) for t, x in zip(ts, fed)]
        dreads = [jnp.where(masks[1] > 0, dot1(og, u, NT), 0.0).astype(BF16) for og, u in zip(ogs, us)]
        kms = [(k * down).astype(BF16) for k, down in zip(ks, downs)]
        qus = [(q * up).astype(BF16) for q, up in zip(qs, ups)]
        dqus = [dot1(x, km) for x, km in zip(dreads, kms)]
        dqs = [x * up + y * up0 for x, up, y, up0 in zip(dqus, ups, crossed, ups0)]
        dkms = [dot1(x, qu, TN) for x, qu in zip(dreads, qus)]
        ggs = [qu.astype(F32) * x + q * up0 * y for qu, x, q, up0, y in zip(qus, dqus, qs, ups0, crossed)]
        dmix = [unnorm(n, scale, dq * DK ** (-0.5)) * slope for n, scale, dq, slope in zip(normed, scales, dqs, slopes)]
        raw = [shift_back(0, lane, x) for lane, x in zip(lanes, dmix)]
        for h, lane, u, wlocal, km, g, (main, over) in zip(heads, lanes, us, wls, dkms, ggs, raw):
            uu[h], wl[h], dkm[h], gg[h] = u, wlocal, km, g
            keep(0, lane, main, over)
        return carry

    def spill_copy(at):
        p, first, width = ((0, 0, 1024), (1, 0, 512), (1, 512, 512))[at]
        block = (pl.ds(p, min(p + 1, 2)), slice(None), pl.ds(first, width))
        return pltpu.make_async_remote_copy(
            src_ref=spill.at[block], dst_ref=spill_in.at[block], send_sem=sp_sem.at[at, 0],
            recv_sem=sp_sem.at[at, 1], device_id=(before, head), device_id_type=MESH,
        )

    def add_spill(p, first, width, axis):
        at = pl.ds(first, width)
        low = tail[p, 8:16, at] + spill_in[p, :, at]
        own[p, TOK - HALO :, at] = jnp.concatenate([tail[p, 0:8, at], low], axis=0).astype(BF16)
        raws[p, tokens(spot[axis]), at] = own[p, :, at]

    def along(axis, step, other=0):
        to = lax.rem(core + other, 2)
        if axis == 0:
            return (row * ROW + lax.rem(z + step, 4) * 2 + to, head)
        return (lax.rem(row + step, 4) * ROW + z * 2 + to, head)

    def gather(unit, kind):
        p, first, width, axis = UNITS[unit]
        off = (0, 0, 3, 1, 0, 3, 1, 2)[kind]
        if kind == 2:
            at = pl.ds(first, width // 2)
        elif kind == 3:
            at = pl.ds(first + width // 2, width // 2)
        else:
            at = pl.ds(first, width)
        slot = lax.rem((z, row)[axis] + off, 4) * 2 + core
        block = raws.at[p, tokens(slot), at]
        to = along(axis, (1, 3, 1, 3, 0, 0, 0, 0)[kind], kind // 4)
        return pltpu.make_async_remote_copy(
            src_ref=block, dst_ref=block, send_sem=a_ssem.at[unit, kind], recv_sem=a_rsem.at[unit, kind],
            device_id=to, device_id_type=MESH,
        )

    def set_out(unit):
        add_spill(*UNITS[unit])
        for kind in (0, 1, 4):
            gather(unit, kind).start()

    def hand_on(unit):
        gather(unit, 0).wait_recv()
        gather(unit, 2).start()
        gather(unit, 5).start()
        gather(unit, 1).wait_recv()
        gather(unit, 3).start()
        gather(unit, 6).start()

    def part_copy(unit, step):
        p, first, width, axis = UNITS[unit]
        mate = lax.rem((row, z)[axis] + step, ROWS)
        return pltpu.make_async_remote_copy(
            src_ref=psend.at[unit, mate], dst_ref=precv.at[unit, step],
            send_sem=p_ssem.at[unit, step], recv_sem=p_rsem.at[unit, step],
            device_id=along(1 - axis, step), device_id_type=MESH,
        )

    def share(unit):
        gather(unit, 2).wait_recv()
        gather(unit, 3).wait_recv()
        gather(unit, 7).start()

    def finish(unit):
        p, first, width, axis = UNITS[unit]
        for kind in (4, 5, 6, 7):
            gather(unit, kind).wait_recv()
        made = [
            jnp.dot(ht_recv[axis], raws[p, :, first + at : first + at + HALF], preferred_element_type=F32)
            for at in (0, HALF)
        ]
        for piece in range(ROWS):
            rows = slice(piece * SLAB, piece * SLAB + SLAB)
            block = jnp.concatenate([made[0][rows], made[1][rows]], axis=0)
            psend[unit, piece] = block.astype(BF16)
            part[unit, piece] = block
        for step in range(1, ROWS):
            part_copy(unit, step).start()

    def receive(unit):
        p, first, width, axis = UNITS[unit]
        total = part[unit, (row, z)[axis]]
        for step in range(1, ROWS):
            part_copy(unit, step).wait_recv()
            total = total + precv[unit, step].astype(F32)
        wg_ref[p, :, first : first + HALF] = total[:SLAB]
        wg_ref[p, :, first + HALF : first + 2 * HALF] = total[SLAB:]

    def input_part(low, high):
        def one(tile, carry):
            at = pl.ds(pl.multiple_of(tile * 256, 256), 256)
            total = jnp.zeros((TOK, 256), F32) if low == 0 else ipart[:, at]
            for p in range(low, high):
                mine = own[p]
                total = total + lax.dot_general(mine, wbuf[p, at, :], NT, preferred_element_type=F32)
            ipart[:, at] = total
            if high == 3:
                isend[:, at] = total.astype(BF16)
            return carry

        lax.fori_loop(0, D // 256, one, 0)

    def input_copy(step):
        mate = lax.rem(head + step, 4)
        return pltpu.make_async_remote_copy(
            src_ref=isend.at[pl.ds(pl.multiple_of(mate * 32, 32), 32)], dst_ref=irecv.at[step],
            send_sem=i_ssem.at[step], recv_sem=i_rsem.at[step], device_id=(ctx, mate), device_id_type=MESH,
        )

    lax.fori_loop(0, HEADS // 4, local, 0)
    spill_copy(0).start()

    for j in range(ROW):
        @pl.when(j != col)
        def _():
            pltpu.make_async_remote_copy(
                src_ref=mb.at[j], dst_ref=rx.at[j], send_sem=mb_ssem.at[j], recv_sem=mb_rsem.at[j],
                device_id=(row * ROW + j, head), device_id_type=MESH,
            ).wait_recv()

    spill_copy(0).wait_recv()
    set_out(0)
    set_out(1)

    def compose(m, x, b):
        hi, lo = split(x)
        out = jnp.dot(m, jnp.concatenate([hi, lo], axis=1), preferred_element_type=F32)
        n = x.shape[1]
        return out[:, :n] + out[:, n:] + b

    half = ROW // 2
    zeros = jnp.zeros((DK, DK), F32)
    ends = [rx[half - 1].astype(F32), rx[ROW - 1].astype(F32)]
    for j in range(half - 2, -1, -1):
        for k in range(2):
            at = k * half + j
            pc[at] = ends[k]
            b = jnp.concatenate([zeros, rx[at, :, DK:].astype(F32)], axis=1)
            ends[k] = compose(rx[at, :, 0:DK], ends[k], b)
    b = jnp.concatenate([zeros, ends[0][:, DK:]], axis=1)
    tot[...] = (dot3(ends[0][:, 0:DK], ends[1]) + b).astype(BF16)

    def ry_copy(step):
        mate = lax.rem(row + step, ROWS) * ROW + col
        return pltpu.make_async_remote_copy(
            src_ref=tot, dst_ref=ry.at[ROWS - step], send_sem=ry_ssem.at[step], recv_sem=ry_rsem.at[step],
            device_id=(mate, head), device_id_type=MESH,
        )

    for step in range(1, ROWS):
        @pl.when(row + step >= ROWS)
        def _():
            ry_copy(step).start()

    hand_on(0)
    hand_on(1)
    for axis in range(2):
        for step in range(1, ROW):
            ht_copy(axis, step).wait()
    carry_in[...] = zeros
    for k in range(ROWS - 1, 0, -1):
        @pl.when(row + k < ROWS)
        def _():
            ry_copy(ROWS - k).wait_recv()
            carry_in[...] = compose(ry[k, :, 0:DK], carry_in[...], ry[k, :, DK:].astype(F32))

    total = carry_in[...]

    def ds_copy(j):
        return pltpu.make_async_remote_copy(
            src_ref=ds.at[j], dst_ref=rd.at[col], send_sem=ds_ssem.at[j], recv_sem=ds_rsem.at[col],
            device_id=(row * ROW + j, head), device_id_type=MESH,
        )

    middle = dot3(ends[1][:, 0:DK], total) + ends[1][:, DK:]
    entries = [middle.astype(BF16), total.astype(BF16)]
    for j in range(ROW):
        if j % half == half - 1:
            ds[j] = entries[j // half]
        else:
            ds[j] = (dot1(pc[j, :, 0:DK], entries[j // half]) + pc[j, :, DK:]).astype(BF16)
    for step in FAR_FIRST:
        ds_copy(lax.rem(col + step, ROW)).start()
    rd[col] = ds[col]

    share(0)
    share(1)
    finish(0)
    finish(1)
    input_part(0, 1)

    def returned(first, last):
        for j in range(first, last):
            @pl.when(j != col)
            def _():
                pltpu.make_async_remote_copy(
                    src_ref=ds.at[j], dst_ref=rd.at[j], send_sem=ds_ssem.at[j], recv_sem=ds_rsem.at[j],
                    device_id=(row * ROW + j, head), device_id_type=MESH,
                ).wait_recv()

    def carried(step, carry):
        heads = [step * 4 + k for k in range(4)]
        lanes = [pl.ds(pl.multiple_of(h * DK, DK), DK) for h in heads]
        above = (iota(1) >= iota(0)).astype(F32).astype(BF16)
        ones = jnp.ones((8, DK), BF16)
        lead = masks[2]
        ups, downs = [grow[h] for h in heads], [shrink[h] for h in heads]
        firsts, lasts = [edges[h, 0:1] for h in heads], [edges[h, 1:2] for h in heads]
        ks = [norm[1, h] for h in heads]
        nexts = [rd[h] for h in heads]
        states = [s0_ref[0, h] for h in heads]
        us = [uu[h] for h in heads]
        read_dkm, read_gg = [dkm[h] for h in heads], [gg[h] for h in heads]
        slopes = [(dsil[1, h], dsil[2, h]) for h in heads]
        scales = [inv[1, h] for h in heads]
        bws = [bet[h] * (wl[h] + two_pass(tk[h], x)) for h, x in zip(heads, nexts)]
        das = [jnp.where(masks[0] > 0, -dot1(bw, u, NT), 0.0).astype(BF16) for bw, u in zip(bws, us)]
        olds = [dot1(bw * lead, state, NT) * e for bw, state, e in zip(bws, states, firsts)]
        kms = [(k * down).astype(BF16) for k, down in zip(ks, downs)]
        kus = [(k * up).astype(BF16) for k, up in zip(ks, ups)]
        dkus = [dot1(da, km) for da, km in zip(das, kms)]
        dkms = [x + dot1(da, ku, TN) for x, da, ku in zip(read_dkm, das, kus)]
        dends = [dot1(u, x, NT) * e * masks[3] for u, x, e in zip(us, nexts, lasts)]
        risings = [(x - old) * up for x, old, up in zip(dkus, olds, ups)]
        endings = [x * down for x, down in zip(dends, downs)]
        fallings = [x * down + y for x, down, y in zip(dkms, downs, endings)]
        dmix = [
            unnorm(k, scale, x + y) * slope[0]
            for k, scale, x, y, slope in zip(ks, scales, risings, fallings, slopes)
        ]
        raw1 = [shift_back(1, lane, x) for lane, x in zip(lanes, dmix)]
        raw2 = [shift_back(2, lane, bw * slope[1]) for lane, bw, slope in zip(lanes, bws, slopes)]
        for lane, one, two in zip(lanes, raw1, raw2):
            keep(1, lane, *one)
            keep(2, lane, *two)
        dgs = [
            g + ku.astype(F32) * x - km.astype(F32) * y - k * (old * up + end)
            for g, ku, x, km, y, k, old, up, end in zip(read_gg, kus, dkus, kms, dkms, ks, olds, ups, endings)
        ]
        crossed = [split(state * x.astype(F32) * lead_last) for state, x in zip(states, nexts)]
        extras = [dot1(ones, ch, NT) + dot1(ones, cl, NT) for ch, cl in crossed]
        extras = [
            x[0:1] * e * last + jnp.sum(k * y, axis=0, keepdims=True)
            for x, e, last, k, y in zip(extras, firsts, lasts, ks, endings)
        ]
        dlds = [dot_exact_left(above, dg) + x for dg, x in zip(dgs, extras)]
        for lane, x in zip(lanes, dlds):
            dld_ref[:, lane] = x
        return carry

    returned(0, 4)
    carried(0, 0)
    spill_copy(1).start()
    returned(4, 8)
    carried(1, 0)
    spill_copy(2).start()
    spill_copy(1).wait_recv()
    set_out(2)
    set_out(3)
    spill_copy(2).wait_recv()
    set_out(4)
    set_out(5)
    hand_on(2)
    hand_on(3)
    input_part(1, 3)
    for step in range(1, 4):
        input_copy(step).start()
    hand_on(4)
    hand_on(5)
    share(2)
    share(3)
    finish(2)
    finish(3)
    share(4)
    share(5)
    receive(0)
    receive(1)
    finish(4)
    finish(5)
    for step in range(1, 4):
        input_copy(step).wait_recv()
    total = ipart[pl.ds(pl.multiple_of(head * 32, 32), 32), :]
    for step in range(1, 4):
        total = total + irecv[step].astype(F32)
    ig_ref[...] = total.astype(BF16)
    for unit in range(2, len(UNITS)):
        receive(unit)

    for at in range(3):
        spill_copy(at).wait_send()
    for step in range(1, ROWS):
        input_copy(step).wait_send()

        @pl.when(row + step >= ROWS)
        def _():
            ry_copy(step).wait_send()

    for j in range(ROW):
        @pl.when(j != col)
        def _():
            mb_copy(j).wait_send()
            ds_copy(j).wait_send()
    for unit in range(len(UNITS)):
        for kind in range(8):
            gather(unit, kind).wait_send()
        for step in range(1, ROWS):
            part_copy(unit, step).wait_send()


def chain(doc_lengths, hidden, proj_weight, conv_weight, log_decay, write_beta, saved_state, output_grad):
    vm = pl.BlockSpec(memory_space=pltpu.VMEM)
    hbm = pl.BlockSpec(memory_space=pl.ANY)
    sq = (HEADS, TOK, DK)
    dma = pltpu.SemaphoreType.DMA
    return pl.pallas_call(
        chain_kernel,
        out_shape=(
            jax.ShapeDtypeStruct((3, SLAB, HEADS * DK), F32),
            jax.ShapeDtypeStruct((32, D), BF16),
            jax.ShapeDtypeStruct((TOK, HEADS * DK), F32),
        ),
        in_specs=[pl.BlockSpec(memory_space=pltpu.SMEM), vm, hbm, vm, hbm, vm, hbm, hbm],
        out_specs=(vm, vm, vm),
        scratch_shapes=[
            pltpu.VMEM((TOK, HEADS * DK), F32),
            pltpu.VMEM((1,) + sq, F32),
            pltpu.VMEM((TOK, HEADS * DK), BF16),
            pltpu.VMEM((HALO + TOK, D), BF16),
            pltpu.VMEM((3, D, HEADS * DK), BF16),
            pltpu.VMEM((3, HALO + TOK, HEADS * DK), F32),
            pltpu.VMEM((D, TOK), F32),
            pltpu.VMEM((2, ROW, ROWS * SLAB, TOK), BF16),
            pltpu.VMEM((2, ROWS * SLAB, ROW * TOK), BF16),
            pltpu.VMEM((2,) + sq, F32),
            pltpu.VMEM(sq, F32),
            pltpu.VMEM((2,) + sq, F32),
            pltpu.VMEM((3,) + sq, F32),
            pltpu.VMEM((7, TOK, TOK), F32),
            pltpu.VMEM(sq, F32),
            pltpu.VMEM(sq, F32),
            pltpu.VMEM(sq, F32),
            pltpu.VMEM((HEADS, 8, DK), F32),
            pltpu.VMEM(sq, F32),
            pltpu.VMEM(sq, BF16),
            pltpu.VMEM((HEADS, DK, 2 * DK), BF16),
            pltpu.VMEM((ROW, DK, 2 * DK), BF16),
            pltpu.VMEM((ROW, DK, 2 * DK), F32),
            pltpu.VMEM((DK, 2 * DK), BF16),
            pltpu.VMEM((ROWS, DK, 2 * DK), BF16),
            pltpu.VMEM((DK, DK), F32),
            pltpu.VMEM((ROW, DK, DK), BF16),
            pltpu.VMEM((HEADS, DK, DK), BF16),
            pltpu.VMEM(sq, BF16),
            pltpu.VMEM(sq, F32),
            pltpu.VMEM(sq, F32),
            pltpu.VMEM(sq, F32),
            pltpu.VMEM(sq, F32),
            pltpu.VMEM((3, HALO, HEADS * DK), F32),
            pltpu.VMEM((3, 8, HEADS * DK), F32),
            pltpu.VMEM((3, 8, HEADS * DK), F32),
            pltpu.VMEM((3, TOK, HEADS * DK), BF16),
            pltpu.VMEM((3, ROW * TOK, HEADS * DK), BF16),
            pltpu.VMEM((len(UNITS), ROWS, 2 * SLAB, HALF), F32),
            pltpu.VMEM((len(UNITS), ROWS, 2 * SLAB, HALF), BF16),
            pltpu.VMEM((len(UNITS), ROWS, 2 * SLAB, HALF), BF16),
            pltpu.VMEM((TOK, D), F32),
            pltpu.VMEM((TOK, D), BF16),
            pltpu.VMEM((4, 32, D), BF16),
            dma((3,)), dma((4,)), dma, dma((2,)), dma((2, ROW)), dma((2, ROW)), dma((ROW,)), dma((ROW,)),
            dma((ROWS,)), dma((ROWS,)), dma((ROW,)), dma((ROW,)), dma((3, 2)),
            dma((len(UNITS), 8)), dma((len(UNITS), 8)), dma((len(UNITS), ROWS)), dma((len(UNITS), ROWS)), dma((4,)), dma((4,)),
        ],
        compiler_params=pltpu.CompilerParams(
            collective_id=0, has_side_effects=True, vmem_limit_bytes=56 * 1024 * 1024
        ),
        cost_estimate=pl.CostEstimate(flops=8_000_000_000, bytes_accessed=18_000_000, transcendentals=1_000_000),
        name="chain",
    )(doc_lengths, hidden, proj_weight, conv_weight, log_decay, write_beta.T, saved_state, output_grad)


def settle_kernel(wg_ref, ig_ref, dld_ref, wg_out, ig_out, dld_out, wg, ig, dld, sems):
    moves = ((wg_ref, wg, wg_out), (dld_ref, dld, dld_out), (ig_ref, ig, ig_out))
    inward = [pltpu.make_async_copy(src, mid, sems.at[0, k]) for k, (src, mid, dst) in enumerate(moves)]
    outward = [pltpu.make_async_copy(mid, dst, sems.at[1, k]) for k, (src, mid, dst) in enumerate(moves)]
    for copy in inward:
        copy.start()
    for arrived, copy in zip(inward, outward):
        arrived.wait()
        copy.start()
    for copy in outward:
        copy.wait()


def settle(*arrays):
    anywhere = pl.BlockSpec(memory_space=pl.ANY)
    return pl.pallas_call(
        settle_kernel,
        out_shape=tuple(jax.ShapeDtypeStruct(a.shape, a.dtype) for a in arrays),
        in_specs=[anywhere] * 3,
        out_specs=(anywhere,) * 3,
        scratch_shapes=[pltpu.VMEM(a.shape, a.dtype) for a in arrays] + [pltpu.SemaphoreType.DMA((2, 3))],
        name="settle",
    )(*arrays)


def body(hidden, proj_weight, conv_weight, log_decay, write_beta, saved_state, output_grad, doc_lengths):
    weight_grads, input_grad, decay_grad = settle(
        *chain(doc_lengths, hidden, proj_weight, conv_weight, log_decay, write_beta, saved_state, output_grad)
    )
    return (jnp.transpose(weight_grads, (1, 0, 2)), input_grad, decay_grad)


def solution(mesh):
    return jax.shard_map(
        body,
        mesh=mesh,
        in_specs=(
            P("ctx", None),
            P(None, None, "head"),
            P(None, None, "head"),
            P("ctx", "head"),
            P("ctx", "head"),
            P("ctx", "head", None, None),
            P("ctx", "head"),
            P(),
        ),
        out_specs=(P("ctx", None, "head"), P(("ctx", "head"), None), P("ctx", "head")),
        check_vma=False,
    )
```

```python
import functools

import jax
import jax.numpy as jnp
from jax import lax
from jax.experimental import pallas as pl
from jax.experimental.pallas import tpu as pltpu
from jax.sharding import PartitionSpec as P

MESH = pl.DeviceIdType.MESH
F32, BF16 = jnp.float32, jnp.bfloat16
EPSILON = 1e-06
HEADS, TOK, DK, D = 8, 128, 128, 2304
ROW, ROWS = 8, 4
SLAB, HALF = 72, 256
HALO = 16
NN, NT, TN = (((1,), (0,)), ((), ())), (((1,), (1,)), ((), ())), (((0,), (0,)), ((), ()))


def dot1(a, b, form=NN):
    return lax.dot_general(a.astype(BF16), b.astype(BF16), form, preferred_element_type=F32)


def split(a):
    high = a.astype(BF16)
    return high, (a - high.astype(F32)).astype(BF16)


def dot3(a, b, form=NN):
    (ah, al), (bh, bl) = split(a), split(b)
    (la,), (lb,) = form[0]
    left = jnp.concatenate([ah, al, ah], axis=la)
    right = jnp.concatenate([bh, bh, bl], axis=lb)
    return lax.dot_general(left, right, form, preferred_element_type=F32)


def two_pass(a, b):
    ah, al = split(a)
    return lax.dot_general(
        jnp.concatenate([ah, al], axis=1), jnp.concatenate([b, b], axis=0), NN, preferred_element_type=F32
    )


def dot_exact_left(a, b):
    bh, bl = split(b)
    return lax.dot_general(
        jnp.concatenate([a, a], axis=1), jnp.concatenate([bh, bl], axis=0), NN, preferred_element_type=F32
    )


def iota(dim):
    return lax.broadcasted_iota(jnp.int32, (TOK, TOK), dim)


def me():
    return lax.axis_index("ctx"), lax.axis_index("head")


UNITS = ((0, 0, 512, 0), (0, 512, 512, 1), (1, 0, 512, 0), (2, 0, 512, 1), (1, 512, 512, 0), (2, 512, 512, 1))
FAR_FIRST = (4, 5, 3, 2, 6, 7, 1)


def chain_kernel(
    doc_ref, hid_ref, w_ref, conv_ref, ld_hbm, beta_ref, s0_hbm, og_hbm,
    wg_ref, ig_ref, dld_ref,
    ld_ref, s0_ref, og_ref, xext, wbuf, pe, ht_t, ht_send, ht_recv, norm, val, inv, dsil, masks, bet,
    grow, shrink, edges, tinv, read, mb, rx, pc, tot, ry, carry_in, ds, rd, uu, wl, tk, dkm, gg,
    tail, spill, spill_in, own, raws, part, psend, precv, ipart, isend, irecv,
    in_sem, w_sem, x_sem, halo_sem, ht_ssem, ht_rsem, mb_ssem, mb_rsem, ry_ssem, ry_rsem, ds_ssem, ds_rsem, sp_sem,
    a_ssem, a_rsem, p_ssem, p_rsem, i_ssem, i_rsem,
):
    ctx, head = me()
    row, col = ctx // ROW, lax.rem(ctx, ROW)
    z, core = col // 2, lax.rem(col, 2)
    place = row * 2 + core
    after, before = lax.rem(ctx + 1, ROW * ROWS), lax.rem(ctx + ROW * ROWS - 1, ROW * ROWS)

    def w_copy(group):
        at = pl.ds(pl.multiple_of(group * 256, 256), 256)
        return pltpu.make_async_copy(w_ref.at[:, :, at], wbuf.at[:, :, at], w_sem.at[group])

    late = [
        pltpu.make_async_copy(src, dst, in_sem.at[k])
        for k, (src, dst) in enumerate(((ld_hbm, ld_ref), (og_hbm, og_ref), (s0_hbm, s0_ref)))
    ]
    late[0].start()
    for group in range(4):
        w_copy(group).start()
    for copy in late[1:]:
        copy.start()
    x_copy = pltpu.make_async_copy(hid_ref, xext.at[pl.ds(HALO, TOK)], x_sem)
    x_copy.start()

    barrier = pltpu.get_barrier_semaphore()
    for step in range(1, ROW):
        mate = row * ROW + lax.rem(col + step, ROW)
        pl.semaphore_signal(barrier, inc=1, device_id=(mate, head), device_id_type=MESH)
    for step in range(1, ROW):
        mate = lax.rem(place + step, ROW)
        mate = mate // 2 * ROW + z * 2 + lax.rem(mate, 2)
        pl.semaphore_signal(barrier, inc=1, device_id=(mate, head), device_id_type=MESH)
    for step in range(1, 4):
        pl.semaphore_signal(barrier, inc=1, device_id=(ctx, lax.rem(head + step, 4)), device_id_type=MESH)
    for mate in (after, before):
        pl.semaphore_signal(barrier, inc=1, device_id=(mate, head), device_id_type=MESH)

    t, s = iota(0), iota(1)
    first = ctx * TOK
    seg_t, seg_s = jnp.zeros_like(t), jnp.zeros_like(s)
    seg_last, start = jnp.int32(0), jnp.int32(0)
    for doc in range(8):
        seg_t = jnp.where(t + first >= start, jnp.maximum(seg_t, start), seg_t)
        seg_s = jnp.where(s + first >= start, jnp.maximum(seg_s, start), seg_s)
        seg_last = jnp.where(first + TOK - 1 >= start, jnp.maximum(seg_last, start), seg_last)
        start = start + doc_ref[doc]
    same = seg_t == seg_s
    masks[0] = jnp.where(same & (t > s), 1.0, 0.0)
    masks[1] = jnp.where(same & (t >= s), 1.0, 0.0)
    masks[2] = jnp.where(seg_t < first, 1.0, 0.0)
    masks[3] = jnp.where(seg_t == seg_last, 1.0, 0.0)
    for offset in range(1, 4):
        masks[3 + offset] = jnp.where(t + first - offset >= seg_t, 1.0, 0.0)
    lead_last = jnp.where(seg_last < first, 1.0, 0.0)
    for h in range(HEADS):
        bet[h] = jnp.broadcast_to(beta_ref[h : h + 1, :], (TOK, TOK)).T

    pl.semaphore_wait(barrier, 2 * (ROW - 1) + 3 + 2)

    halo = pltpu.make_async_remote_copy(
        src_ref=hid_ref.at[pl.ds(TOK - HALO, HALO)], dst_ref=xext.at[pl.ds(0, HALO)],
        send_sem=halo_sem.at[0], recv_sem=halo_sem.at[1], device_id=(after, head), device_id_type=MESH,
    )
    halo.start()

    for tile in range(D // 128):
        ht_t[tile * 128 : tile * 128 + 128] = hid_ref[:, tile * 128 : tile * 128 + 128].astype(F32).T
    for axis in range(2):
        for owner in range(ROW):
            slabs = [
                (piece * ROW + owner, owner // 2 * ROW + piece * 2 + owner % 2)[axis] for piece in range(ROWS)
            ]
            rows = [ht_t[slab * SLAB : slab * SLAB + SLAB] for slab in slabs]
            ht_send[axis, owner] = jnp.concatenate(rows, axis=0).astype(BF16)
    spot = (col, place)

    def tokens(j):
        return pl.ds(pl.multiple_of(j * TOK, TOK), TOK)

    def ht_copy(axis, step):
        mate = lax.rem(spot[axis] + step, ROW)
        device = (row * ROW + mate, mate // 2 * ROW + z * 2 + lax.rem(mate, 2))[axis]
        return pltpu.make_async_remote_copy(
            src_ref=ht_send.at[axis, mate], dst_ref=ht_recv.at[axis, :, tokens(spot[axis])],
            send_sem=ht_ssem.at[axis, step], recv_sem=ht_rsem.at[axis, step],
            device_id=(device, head), device_id_type=MESH,
        )

    for step in range(1, ROW):
        for axis in range(2):
            ht_copy(axis, step).start()
    for axis in range(2):
        ht_recv[axis, :, tokens(spot[axis])] = ht_send[axis, spot[axis]]

    below = (iota(0) >= iota(1)).astype(F32).astype(BF16)
    late[0].wait()
    for h in range(HEADS):
        summed = dot_exact_left(below, ld_ref[:, h * DK : h * DK + DK])
        mid = summed[63:64]
        grow[h], shrink[h] = jnp.exp(summed - mid), jnp.exp(mid - summed)
        edges[h, 0:1], edges[h, 1:2] = jnp.exp(mid), jnp.exp(summed[TOK - 1 :] - mid)

    x_copy.wait()
    halo.wait()

    def project(group, carry):
        w_copy(group).wait()
        wide = pl.ds(pl.multiple_of(group * 256, 256), 256)
        for p in range(3):
            made = jnp.dot(xext[...], wbuf[p, :, wide], preferred_element_type=F32)
            pe[p, :, wide] = made.astype(BF16).astype(F32)
        for half in range(2):
            h = group * 2 + half
            lanes = pl.ds(pl.multiple_of(h * DK, DK), DK)
            for p in range(3):
                mixed = pe[p, pl.ds(HALO, TOK), lanes] * conv_ref[p, 0:1, lanes]
                for offset in range(1, 4):
                    tap = pe[p, pl.ds(HALO - offset, TOK), lanes] * conv_ref[p, offset : offset + 1, lanes]
                    mixed = mixed + tap * masks[3 + offset]
                gate = 1.0 / (1.0 + jnp.exp(-mixed))
                active = mixed * gate
                dsil[p, h] = gate * (1.0 + mixed * (1.0 - gate))
                if p == 2:
                    val[h] = active
                else:
                    scale = lax.rsqrt(jnp.sum(active * active, axis=1, keepdims=True) + EPSILON)
                    norm[p, h] = active * scale
                    inv[p, h] = jnp.broadcast_to(scale, (TOK, DK))
        return carry

    lax.fori_loop(0, 4, project, 0)

    def mb_copy(h):
        return pltpu.make_async_remote_copy(
            src_ref=mb.at[h], dst_ref=rx.at[col], send_sem=mb_ssem.at[h], recv_sem=mb_rsem.at[col],
            device_id=(row * ROW + h, head), device_id_type=MESH,
        )

    batch = 8

    def transition(step, carry):
        heads = [step * batch + k for k in range(batch)]
        lanes = [pl.ds(pl.multiple_of(h * DK, DK), DK) for h in heads]
        ups, downs = [grow[h] for h in heads], [shrink[h] for h in heads]
        firsts, lasts = [edges[h, 0:1] for h in heads], [edges[h, 1:2] for h in heads]
        betas = [bet[h] for h in heads]
        grads_out = [og_ref[:, lane] for lane in lanes]
        keys = [norm[1, h] for h in heads]
        queries = [norm[0, h] * DK ** (-0.5) for h in heads]
        low = [k * x for k, x in zip(keys, downs)]
        high = [jnp.concatenate([k * x, q * x], axis=0) for k, q, x in zip(keys, queries, ups)]
        both = [dot3(a, b, NT) for a, b in zip(high, low)]
        ns = [jnp.where(masks[0] > 0, x[:TOK], 0.0) * b for x, b in zip(both, betas)]
        rs = [jnp.where(masks[1] > 0, x[TOK:], 0.0) for x in both]
        apart = iota(0) ^ iota(1)
        eye = (apart == 0).astype(F32)
        solved = [eye - jnp.where(apart == 1, n, 0.0) for n in ns]
        for level in range(1, 7):
            edge = [jnp.where((apart >> level) == 1, n, 0.0) for n in ns]
            edge = [dot3(e, x) for e, x in zip(edge, solved)]
            solved = [x - dot3(x, e) for e, x in zip(edge, solved)]
        lead = masks[2]
        ups0 = [x * e * lead for x, e in zip(ups, firsts)]
        ws = [dot3(x, b * k * up) for x, b, k, up in zip(solved, betas, keys, ups0)]
        xs = [q * up - dot1(r, w) for q, up, r, w in zip(queries, ups0, rs, ws)]
        ends = [x * last * masks[3] for x, last in zip(low, lasts)]
        moves = [
            (eye * (last * e * lead_last) - dot1(w, end, TN)).astype(BF16)
            for w, end, last, e in zip(ws, ends, lasts, firsts)
        ]
        owns = [dot1(x, og, TN).astype(BF16) for x, og in zip(xs, grads_out)]
        backs = [dot3(x, end, TN) for x, end in zip(solved, ends)]
        for h, move, own, back, x, r in zip(heads, moves, owns, backs, solved, rs):
            mb[h, :, 0:DK], mb[h, :, DK:] = move, own
            tk[h], tinv[h], read[h] = back, x, r.astype(BF16)
        for step in FAR_FIRST:
            mb_copy(lax.rem(col + step, ROW)).start()
        return carry

    for copy in late[1:]:
        copy.wait()
    lax.fori_loop(0, HEADS // batch, transition, 0)
    rx[col] = mb[col]

    def shift_back(p, lane, dmix):
        t = iota(0)
        main = dmix * conv_ref[p, 0:1, lane]
        over = jnp.zeros((TOK, DK), F32)
        for offset in range(1, 4):
            shifted = dmix * masks[3 + offset] * conv_ref[p, offset : offset + 1, lane]
            shifted = pltpu.roll(shifted, TOK - offset, 0)
            inside = t < TOK - offset
            main = main + jnp.where(inside, shifted, 0.0)
            over = over + jnp.where(inside, 0.0, shifted)
        return main, over

    def keep(p, lane, main, over):
        own[p, :, lane] = main.astype(BF16)
        tail[p, :, lane] = main[TOK - HALO :]
        spill[p, :, lane] = over[TOK - 8 :]

    def unnorm(n, scale, grad):
        return scale * (grad - n * jnp.sum(n * grad, axis=1, keepdims=True))

    def local(step, carry):
        heads = [step * 4 + k for k in range(4)]
        lanes = [pl.ds(pl.multiple_of(h * DK, DK), DK) for h in heads]
        ogs = [og_ref[:, lane] for lane in lanes]
        ups, downs = [grow[h] for h in heads], [shrink[h] for h in heads]
        ups0 = [up * edges[h, 0:1] * masks[2] for h, up in zip(heads, ups)]
        normed = [norm[0, h] for h in heads]
        qs = [n * DK ** (-0.5) for n in normed]
        ks = [norm[1, h] for h in heads]
        states = [s0_ref[0, h] for h in heads]
        ts = [tinv[h] for h in heads]
        slopes, scales = [dsil[0, h] for h in heads], [inv[0, h] for h in heads]
        recalled = [dot3(k * up, state) for k, up, state in zip(ks, ups0, states)]
        fed = [dot1(read[h], og, TN) for h, og in zip(heads, ogs)]
        crossed = [dot1(og, state, NT) for og, state in zip(ogs, states)]
        wanted = [bet[h] * (val[h] - x) for h, x in zip(heads, recalled)]
        us = [dot3(t, x).astype(BF16) for t, x in zip(ts, wanted)]
        wls = [dot3(t, x, TN) for t, x in zip(ts, fed)]
        dreads = [jnp.where(masks[1] > 0, dot1(og, u, NT), 0.0).astype(BF16) for og, u in zip(ogs, us)]
        kms = [(k * down).astype(BF16) for k, down in zip(ks, downs)]
        qus = [(q * up).astype(BF16) for q, up in zip(qs, ups)]
        dqus = [dot1(x, km) for x, km in zip(dreads, kms)]
        dqs = [x * up + y * up0 for x, up, y, up0 in zip(dqus, ups, crossed, ups0)]
        dkms = [dot1(x, qu, TN) for x, qu in zip(dreads, qus)]
        ggs = [qu.astype(F32) * x + q * up0 * y for qu, x, q, up0, y in zip(qus, dqus, qs, ups0, crossed)]
        dmix = [unnorm(n, scale, dq * DK ** (-0.5)) * slope for n, scale, dq, slope in zip(normed, scales, dqs, slopes)]
        raw = [shift_back(0, lane, x) for lane, x in zip(lanes, dmix)]
        for h, lane, u, wlocal, km, g, (main, over) in zip(heads, lanes, us, wls, dkms, ggs, raw):
            uu[h], wl[h], dkm[h], gg[h] = u, wlocal, km, g
            keep(0, lane, main, over)
        return carry

    def spill_copy(at):
        p, first, width = ((0, 0, 1024), (1, 0, 512), (1, 512, 512))[at]
        block = (pl.ds(p, min(p + 1, 2)), slice(None), pl.ds(first, width))
        return pltpu.make_async_remote_copy(
            src_ref=spill.at[block], dst_ref=spill_in.at[block], send_sem=sp_sem.at[at, 0],
            recv_sem=sp_sem.at[at, 1], device_id=(before, head), device_id_type=MESH,
        )

    def add_spill(p, first, width, axis):
        at = pl.ds(first, width)
        low = tail[p, 8:16, at] + spill_in[p, :, at]
        own[p, TOK - HALO :, at] = jnp.concatenate([tail[p, 0:8, at], low], axis=0).astype(BF16)
        raws[p, tokens(spot[axis]), at] = own[p, :, at]

    def along(axis, step, other=0):
        to = lax.rem(core + other, 2)
        if axis == 0:
            return (row * ROW + lax.rem(z + step, 4) * 2 + to, head)
        return (lax.rem(row + step, 4) * ROW + z * 2 + to, head)

    def gather(unit, kind):
        p, first, width, axis = UNITS[unit]
        off = (0, 0, 3, 1, 0, 3, 1, 2)[kind]
        if kind == 2:
            at = pl.ds(first, width // 2)
        elif kind == 3:
            at = pl.ds(first + width // 2, width // 2)
        else:
            at = pl.ds(first, width)
        slot = lax.rem((z, row)[axis] + off, 4) * 2 + core
        block = raws.at[p, tokens(slot), at]
        to = along(axis, (1, 3, 1, 3, 0, 0, 0, 0)[kind], kind // 4)
        return pltpu.make_async_remote_copy(
            src_ref=block, dst_ref=block, send_sem=a_ssem.at[unit, kind], recv_sem=a_rsem.at[unit, kind],
            device_id=to, device_id_type=MESH,
        )

    def set_out(unit):
        add_spill(*UNITS[unit])
        for kind in (0, 1, 4):
            gather(unit, kind).start()

    def hand_on(unit):
        gather(unit, 0).wait_recv()
        gather(unit, 2).start()
        gather(unit, 5).start()
        gather(unit, 1).wait_recv()
        gather(unit, 3).start()
        gather(unit, 6).start()

    def part_copy(unit, step):
        p, first, width, axis = UNITS[unit]
        mate = lax.rem((row, z)[axis] + step, ROWS)
        return pltpu.make_async_remote_copy(
            src_ref=psend.at[unit, mate], dst_ref=precv.at[unit, step],
            send_sem=p_ssem.at[unit, step], recv_sem=p_rsem.at[unit, step],
            device_id=along(1 - axis, step), device_id_type=MESH,
        )

    def share(unit):
        gather(unit, 2).wait_recv()
        gather(unit, 3).wait_recv()
        gather(unit, 7).start()

    def finish(unit):
        p, first, width, axis = UNITS[unit]
        for kind in (4, 5, 6, 7):
            gather(unit, kind).wait_recv()
        made = [
            jnp.dot(ht_recv[axis], raws[p, :, first + at : first + at + HALF], preferred_element_type=F32)
            for at in (0, HALF)
        ]
        for piece in range(ROWS):
            rows = slice(piece * SLAB, piece * SLAB + SLAB)
            block = jnp.concatenate([made[0][rows], made[1][rows]], axis=0)
            psend[unit, piece] = block.astype(BF16)
            part[unit, piece] = block
        for step in (2, 1, 3):
            part_copy(unit, step).start()

    def receive(unit):
        p, first, width, axis = UNITS[unit]
        total = part[unit, (row, z)[axis]]
        for step in range(1, ROWS):
            part_copy(unit, step).wait_recv()
            total = total + precv[unit, step].astype(F32)
        wg_ref[p, :, first : first + HALF] = total[:SLAB]
        wg_ref[p, :, first + HALF : first + 2 * HALF] = total[SLAB:]

    def input_part(low, high, first, width):
        cols = slice(first, first + width)

        def one(tile, carry):
            at = pl.ds(pl.multiple_of(tile * 256, 256), 256)
            total = jnp.zeros((TOK, 256), F32) if low == 0 else ipart[:, at]
            for p in range(low, high):
                total = total + lax.dot_general(own[p, :, cols], wbuf[p, at, cols], NT, preferred_element_type=F32)
            ipart[:, at] = total
            if first > 0:
                isend[:, at] = total.astype(BF16)
            return carry

        lax.fori_loop(0, D // 256, one, 0)

    def input_copy(step):
        mate = lax.rem(head + step, 4)
        return pltpu.make_async_remote_copy(
            src_ref=isend.at[pl.ds(pl.multiple_of(mate * 32, 32), 32)], dst_ref=irecv.at[step],
            send_sem=i_ssem.at[step], recv_sem=i_rsem.at[step], device_id=(ctx, mate), device_id_type=MESH,
        )

    lax.fori_loop(0, HEADS // 4, local, 0)
    spill_copy(0).start()

    for j in range(ROW):
        @pl.when(j != col)
        def _():
            pltpu.make_async_remote_copy(
                src_ref=mb.at[j], dst_ref=rx.at[j], send_sem=mb_ssem.at[j], recv_sem=mb_rsem.at[j],
                device_id=(row * ROW + j, head), device_id_type=MESH,
            ).wait_recv()

    spill_copy(0).wait_recv()
    set_out(0)
    set_out(1)

    def compose(m, x, b):
        hi, lo = split(x)
        out = jnp.dot(m, jnp.concatenate([hi, lo], axis=1), preferred_element_type=F32)
        n = x.shape[1]
        return out[:, :n] + out[:, n:] + b

    half = ROW // 2
    zeros = jnp.zeros((DK, DK), F32)
    ends = [rx[half - 1].astype(F32), rx[ROW - 1].astype(F32)]
    for j in range(half - 2, -1, -1):
        for k in range(2):
            at = k * half + j
            pc[at] = ends[k]
            b = jnp.concatenate([zeros, rx[at, :, DK:].astype(F32)], axis=1)
            ends[k] = compose(rx[at, :, 0:DK], ends[k], b)
    b = jnp.concatenate([zeros, ends[0][:, DK:]], axis=1)
    tot[...] = (dot3(ends[0][:, 0:DK], ends[1]) + b).astype(BF16)

    def ry_copy(step):
        mate = lax.rem(row + step, ROWS) * ROW + col
        return pltpu.make_async_remote_copy(
            src_ref=tot, dst_ref=ry.at[ROWS - step], send_sem=ry_ssem.at[step], recv_sem=ry_rsem.at[step],
            device_id=(mate, head), device_id_type=MESH,
        )

    for step in range(1, ROWS):
        @pl.when(row + step >= ROWS)
        def _():
            ry_copy(step).start()

    hand_on(0)
    hand_on(1)
    for axis in range(2):
        for step in range(1, ROW):
            ht_copy(axis, step).wait()
    carry_in[...] = zeros
    for k in range(ROWS - 1, 0, -1):
        @pl.when(row + k < ROWS)
        def _():
            ry_copy(ROWS - k).wait_recv()
            carry_in[...] = compose(ry[k, :, 0:DK], carry_in[...], ry[k, :, DK:].astype(F32))

    total = carry_in[...]

    def ds_copy(j):
        return pltpu.make_async_remote_copy(
            src_ref=ds.at[j], dst_ref=rd.at[col], send_sem=ds_ssem.at[j], recv_sem=ds_rsem.at[col],
            device_id=(row * ROW + j, head), device_id_type=MESH,
        )

    middle = dot3(ends[1][:, 0:DK], total) + ends[1][:, DK:]
    entries = [middle.astype(BF16), total.astype(BF16)]
    for j in range(ROW):
        if j % half == half - 1:
            ds[j] = entries[j // half]
        else:
            ds[j] = (dot1(pc[j, :, 0:DK], entries[j // half]) + pc[j, :, DK:]).astype(BF16)
    for step in FAR_FIRST:
        ds_copy(lax.rem(col + step, ROW)).start()
    rd[col] = ds[col]

    share(0)
    share(1)
    finish(0)
    finish(1)
    input_part(0, 1, 0, 1024)

    def returned(first, last):
        for j in range(first, last):
            @pl.when(j != col)
            def _():
                pltpu.make_async_remote_copy(
                    src_ref=ds.at[j], dst_ref=rd.at[j], send_sem=ds_ssem.at[j], recv_sem=ds_rsem.at[j],
                    device_id=(row * ROW + j, head), device_id_type=MESH,
                ).wait_recv()

    def carried(step, carry):
        heads = [step * 4 + k for k in range(4)]
        lanes = [pl.ds(pl.multiple_of(h * DK, DK), DK) for h in heads]
        above = (iota(1) >= iota(0)).astype(F32).astype(BF16)
        ones = jnp.ones((8, DK), BF16)
        lead = masks[2]
        ups, downs = [grow[h] for h in heads], [shrink[h] for h in heads]
        firsts, lasts = [edges[h, 0:1] for h in heads], [edges[h, 1:2] for h in heads]
        ks = [norm[1, h] for h in heads]
        nexts = [rd[h] for h in heads]
        states = [s0_ref[0, h] for h in heads]
        us = [uu[h] for h in heads]
        read_dkm, read_gg = [dkm[h] for h in heads], [gg[h] for h in heads]
        slopes = [(dsil[1, h], dsil[2, h]) for h in heads]
        scales = [inv[1, h] for h in heads]
        bws = [bet[h] * (wl[h] + two_pass(tk[h], x)) for h, x in zip(heads, nexts)]
        das = [jnp.where(masks[0] > 0, -dot1(bw, u, NT), 0.0).astype(BF16) for bw, u in zip(bws, us)]
        olds = [dot1(bw * lead, state, NT) * e for bw, state, e in zip(bws, states, firsts)]
        kms = [(k * down).astype(BF16) for k, down in zip(ks, downs)]
        kus = [(k * up).astype(BF16) for k, up in zip(ks, ups)]
        dkus = [dot1(da, km) for da, km in zip(das, kms)]
        dkms = [x + dot1(da, ku, TN) for x, da, ku in zip(read_dkm, das, kus)]
        dends = [dot1(u, x, NT) * e * masks[3] for u, x, e in zip(us, nexts, lasts)]
        risings = [(x - old) * up for x, old, up in zip(dkus, olds, ups)]
        endings = [x * down for x, down in zip(dends, downs)]
        fallings = [x * down + y for x, down, y in zip(dkms, downs, endings)]
        dmix = [
            unnorm(k, scale, x + y) * slope[0]
            for k, scale, x, y, slope in zip(ks, scales, risings, fallings, slopes)
        ]
        raw1 = [shift_back(1, lane, x) for lane, x in zip(lanes, dmix)]
        raw2 = [shift_back(2, lane, bw * slope[1]) for lane, bw, slope in zip(lanes, bws, slopes)]
        for lane, one, two in zip(lanes, raw1, raw2):
            keep(1, lane, *one)
            keep(2, lane, *two)
        dgs = [
            g + ku.astype(F32) * x - km.astype(F32) * y - k * (old * up + end)
            for g, ku, x, km, y, k, old, up, end in zip(read_gg, kus, dkus, kms, dkms, ks, olds, ups, endings)
        ]
        crossed = [split(state * x.astype(F32) * lead_last) for state, x in zip(states, nexts)]
        extras = [dot1(ones, ch, NT) + dot1(ones, cl, NT) for ch, cl in crossed]
        extras = [
            x[0:1] * e * last + jnp.sum(k * y, axis=0, keepdims=True)
            for x, e, last, k, y in zip(extras, firsts, lasts, ks, endings)
        ]
        dlds = [dot_exact_left(above, dg) + x for dg, x in zip(dgs, extras)]
        for lane, x in zip(lanes, dlds):
            dld_ref[:, lane] = x
        return carry

    returned(0, 4)
    carried(0, 0)
    spill_copy(1).start()
    returned(4, 8)
    carried(1, 0)
    spill_copy(2).start()
    spill_copy(1).wait_recv()
    set_out(2)
    set_out(3)
    input_part(1, 3, 0, 512)
    spill_copy(2).wait_recv()
    set_out(4)
    set_out(5)
    hand_on(2)
    hand_on(3)
    input_part(1, 3, 512, 512)
    for step in range(1, 4):
        input_copy(step).start()
    hand_on(4)
    hand_on(5)
    share(2)
    share(3)
    finish(2)
    finish(3)
    share(4)
    share(5)
    receive(0)
    receive(1)
    finish(4)
    finish(5)
    for step in range(1, 4):
        input_copy(step).wait_recv()
    total = ipart[pl.ds(pl.multiple_of(head * 32, 32), 32), :]
    for step in range(1, 4):
        total = total + irecv[step].astype(F32)
    ig_ref[...] = total.astype(BF16)
    for unit in range(2, len(UNITS)):
        receive(unit)

    for at in range(3):
        spill_copy(at).wait_send()
    for step in range(1, ROWS):
        input_copy(step).wait_send()

        @pl.when(row + step >= ROWS)
        def _():
            ry_copy(step).wait_send()

    for j in range(ROW):
        @pl.when(j != col)
        def _():
            mb_copy(j).wait_send()
            ds_copy(j).wait_send()
    for unit in range(len(UNITS)):
        for kind in range(8):
            gather(unit, kind).wait_send()
        for step in range(1, ROWS):
            part_copy(unit, step).wait_send()


def chain(doc_lengths, hidden, proj_weight, conv_weight, log_decay, write_beta, saved_state, output_grad):
    vm = pl.BlockSpec(memory_space=pltpu.VMEM)
    hbm = pl.BlockSpec(memory_space=pl.ANY)
    sq = (HEADS, TOK, DK)
    dma = pltpu.SemaphoreType.DMA
    return pl.pallas_call(
        chain_kernel,
        out_shape=(
            jax.ShapeDtypeStruct((3, SLAB, HEADS * DK), F32),
            jax.ShapeDtypeStruct((32, D), BF16),
            jax.ShapeDtypeStruct((TOK, HEADS * DK), F32),
        ),
        in_specs=[pl.BlockSpec(memory_space=pltpu.SMEM), vm, hbm, vm, hbm, vm, hbm, hbm],
        out_specs=(vm, vm, vm),
        scratch_shapes=[
            pltpu.VMEM((TOK, HEADS * DK), F32),
            pltpu.VMEM((1,) + sq, F32),
            pltpu.VMEM((TOK, HEADS * DK), BF16),
            pltpu.VMEM((HALO + TOK, D), BF16),
            pltpu.VMEM((3, D, HEADS * DK), BF16),
            pltpu.VMEM((3, HALO + TOK, HEADS * DK), F32),
            pltpu.VMEM((D, TOK), F32),
            pltpu.VMEM((2, ROW, ROWS * SLAB, TOK), BF16),
            pltpu.VMEM((2, ROWS * SLAB, ROW * TOK), BF16),
            pltpu.VMEM((2,) + sq, F32),
            pltpu.VMEM(sq, F32),
            pltpu.VMEM((2,) + sq, F32),
            pltpu.VMEM((3,) + sq, F32),
            pltpu.VMEM((7, TOK, TOK), F32),
            pltpu.VMEM(sq, F32),
            pltpu.VMEM(sq, F32),
            pltpu.VMEM(sq, F32),
            pltpu.VMEM((HEADS, 8, DK), F32),
            pltpu.VMEM(sq, F32),
            pltpu.VMEM(sq, BF16),
            pltpu.VMEM((HEADS, DK, 2 * DK), BF16),
            pltpu.VMEM((ROW, DK, 2 * DK), BF16),
            pltpu.VMEM((ROW, DK, 2 * DK), F32),
            pltpu.VMEM((DK, 2 * DK), BF16),
            pltpu.VMEM((ROWS, DK, 2 * DK), BF16),
            pltpu.VMEM((DK, DK), F32),
            pltpu.VMEM((ROW, DK, DK), BF16),
            pltpu.VMEM((HEADS, DK, DK), BF16),
            pltpu.VMEM(sq, BF16),
            pltpu.VMEM(sq, F32),
            pltpu.VMEM(sq, F32),
            pltpu.VMEM(sq, F32),
            pltpu.VMEM(sq, F32),
            pltpu.VMEM((3, HALO, HEADS * DK), F32),
            pltpu.VMEM((3, 8, HEADS * DK), F32),
            pltpu.VMEM((3, 8, HEADS * DK), F32),
            pltpu.VMEM((3, TOK, HEADS * DK), BF16),
            pltpu.VMEM((3, ROW * TOK, HEADS * DK), BF16),
            pltpu.VMEM((len(UNITS), ROWS, 2 * SLAB, HALF), F32),
            pltpu.VMEM((len(UNITS), ROWS, 2 * SLAB, HALF), BF16),
            pltpu.VMEM((len(UNITS), ROWS, 2 * SLAB, HALF), BF16),
            pltpu.VMEM((TOK, D), F32),
            pltpu.VMEM((TOK, D), BF16),
            pltpu.VMEM((4, 32, D), BF16),
            dma((3,)), dma((4,)), dma, dma((2,)), dma((2, ROW)), dma((2, ROW)), dma((ROW,)), dma((ROW,)),
            dma((ROWS,)), dma((ROWS,)), dma((ROW,)), dma((ROW,)), dma((3, 2)),
            dma((len(UNITS), 8)), dma((len(UNITS), 8)), dma((len(UNITS), ROWS)), dma((len(UNITS), ROWS)), dma((4,)), dma((4,)),
        ],
        compiler_params=pltpu.CompilerParams(
            collective_id=0, has_side_effects=True, vmem_limit_bytes=56 * 1024 * 1024
        ),
        cost_estimate=pl.CostEstimate(flops=8_000_000_000, bytes_accessed=18_000_000, transcendentals=1_000_000),
        name="chain",
    )(doc_lengths, hidden, proj_weight, conv_weight, log_decay, write_beta.T, saved_state, output_grad)


def settle_kernel(wg_ref, ig_ref, dld_ref, wg_out, ig_out, dld_out, wg, ig, dld, sems):
    moves = ((wg_ref, wg, wg_out), (dld_ref, dld, dld_out), (ig_ref, ig, ig_out))
    inward = [pltpu.make_async_copy(src, mid, sems.at[0, k]) for k, (src, mid, dst) in enumerate(moves)]
    outward = [pltpu.make_async_copy(mid, dst, sems.at[1, k]) for k, (src, mid, dst) in enumerate(moves)]
    for copy in inward:
        copy.start()
    for arrived, copy in zip(inward, outward):
        arrived.wait()
        copy.start()
    for copy in outward:
        copy.wait()


def settle(*arrays):
    anywhere = pl.BlockSpec(memory_space=pl.ANY)
    return pl.pallas_call(
        settle_kernel,
        out_shape=tuple(jax.ShapeDtypeStruct(a.shape, a.dtype) for a in arrays),
        in_specs=[anywhere] * 3,
        out_specs=(anywhere,) * 3,
        scratch_shapes=[pltpu.VMEM(a.shape, a.dtype) for a in arrays] + [pltpu.SemaphoreType.DMA((2, 3))],
        name="settle",
    )(*arrays)


def body(hidden, proj_weight, conv_weight, log_decay, write_beta, saved_state, output_grad, doc_lengths):
    weight_grads, input_grad, decay_grad = settle(
        *chain(doc_lengths, hidden, proj_weight, conv_weight, log_decay, write_beta, saved_state, output_grad)
    )
    return (jnp.transpose(weight_grads, (1, 0, 2)), input_grad, decay_grad)


def solution(mesh):
    return jax.shard_map(
        body,
        mesh=mesh,
        in_specs=(
            P("ctx", None),
            P(None, None, "head"),
            P(None, None, "head"),
            P("ctx", "head"),
            P("ctx", "head"),
            P("ctx", "head", None, None),
            P("ctx", "head"),
            P(),
        ),
        out_specs=(P("ctx", None, "head"), P(("ctx", "head"), None), P("ctx", "head")),
        check_vma=False,
    )
```
